256 devices in a mesh: frame: 64 (over x, z, core), head: 4 (over y).
Axes of the slice: x: 4, y: 4, z: 8, core: 2. Of those that a mesh axis runs over, the one named last changes fastest.
Arguments:
- q_raw: bfloat16 [8192, 5120], P('frame', 'head'), may hold values from -4096 to 4096
- k_raw: bfloat16 [8192, 5120], P('frame', 'head'), may hold values from -4096 to 4096
- v_in: bfloat16 [8192, 5120], P('frame', 'head'), may hold values from -18 to 18
- gain_q: float32 [5120], P('head'), may hold values from 0.5 to 1.5
- gain_k: float32 [5120], P('head'), may hold values from 0.5 to 1.5
- frame_index: int32 [8192], P('frame'), may hold values from 0 to 2, as said below
- reach: int32 [64], P('frame'), may hold values from 0 to 3, as said below
- cotangent: bfloat16 [8192, 5120], P('frame', 'head'), may hold values from -6 to 6
Outputs:
- scaled_out: bfloat16 [8192, 5120], P('frame', 'head')
- grad_q: bfloat16 [8192, 5120], P('frame', 'head')
- grad_k: bfloat16 [8192, 5120], P('frame', 'head')
- grad_v: bfloat16 [8192, 5120], P('frame', 'head')
- grad_gain_q: float32 [5120], P('head')
- grad_gain_k: float32 [5120], P('head')
The draws below stay inside these ranges and needn't reach their ends.
Inputs may be any that keep to these rules, and one draw needn't show every extreme that they name: `frame_index`: within each group of 128 tokens the frame never falls, and all 3 frames are present. reach[c] <= c; reach[1] is 0; the last group has 3.
All inputs are finite; a program needn't handle non-finite values. Where the reference program divides by a largest or mean magnitude, that divisor is 1e-20 or more.
Results may differ from the reference program's by a relative error of at most 0.035.
Values may be sent and summed in bfloat16 or wider, within the bound.
No kernel may reach another device: no remote copies, remote signals or barrier semaphores. Data moves between devices by JAX's collectives and lax.ppermute only.
A program may use at most 64 MiB of HBM per device.

```python
import math
from functools import reduce
import jax
import jax.numpy as jnp
from jax import lax

D = 5120
HEADS = 40
HD = 128
TOK_DEV = 128
LAGS = 3
GROUPS = 64
TOKENS = 8192


def draw_pair(key, align_rate, row_spread):
    normal_q = jax.random.normal(jax.random.fold_in(key, 11), (TOKENS, D), jnp.float32)
    normal_k = jax.random.normal(jax.random.fold_in(key, 12), (TOKENS, D), jnp.float32)
    base_q = jnp.clip(normal_q, -6.0, 6.0)
    base_k = jnp.clip(normal_k, -6.0, 6.0)
    columns = jnp.arange(D, dtype=jnp.float32) / (D - 1)
    col_scale = (1.0 + 2.0 * columns) * jnp.exp(jax.random.uniform(jax.random.fold_in(key, 15), (D,), jnp.float32) * math.log(10.0))
    row_q = jnp.exp(jax.random.uniform(jax.random.fold_in(key, 16), (TOKENS,), jnp.float32) * math.log(row_spread))
    row_k = jnp.exp(jax.random.uniform(jax.random.fold_in(key, 17), (TOKENS,), jnp.float32) * math.log(row_spread))
    raw_q = base_q * col_scale[None, :] * row_q[:, None]
    raw_k = base_k * col_scale[None, :] * row_k[:, None]
    positions = jnp.arange(TOKENS, dtype=jnp.int32)
    chosen = (jax.random.uniform(jax.random.fold_in(key, 18), (TOKENS,), jnp.float32) < align_rate) & (positions % TOK_DEV != 0)
    head_pick = jax.random.randint(jax.random.fold_in(key, 19), (TOKENS,), 0, HEADS)
    strength = 3.0 + 5.0 * jax.random.uniform(jax.random.fold_in(key, 20), (TOKENS,), jnp.float32)
    in_head = jnp.arange(D, dtype=jnp.int32)[None, :] // HD == head_pick[:, None]
    boost = jnp.where(chosen[:, None] & in_head, strength[:, None], 1.0)
    raw_q = raw_q * boost
    nearby = jnp.roll(raw_q * jnp.where(in_head, 0.98, 1.0), -1, axis=0)
    near_chosen = jnp.roll(chosen, -1)
    raw_k = jnp.where(near_chosen[:, None], nearby, raw_k)
    raw_k = jnp.where(chosen[:, None], raw_q, raw_k)
    return (jnp.clip(raw_q, -4096.0, 4096.0), jnp.clip(raw_k, -4096.0, 4096.0))


def draw_q_raw(key, part):
    pair_rows = draw_pair(key, 0.0, 10.0)
    return pair_rows[0].astype(jnp.bfloat16)


def draw_k_raw(key, part):
    pair_rows = draw_pair(key, 0.0, 10.0)
    return pair_rows[1].astype(jnp.bfloat16)


def draw_v_in(key, part):
    key = jax.random.fold_in(key, 31)
    rising = 1.0 + 2.0 * jnp.arange(TOKENS, dtype=jnp.float32) / (TOKENS - 1)
    base_rows = jnp.clip(jax.random.normal(key, (TOKENS, D), jnp.float32), -6.0, 6.0)
    return (base_rows * rising[:, None]).astype(jnp.bfloat16)


def draw_frame_index(key, part):
    key = jax.random.fold_in(key, 41)
    first_cut = jax.random.randint(jax.random.fold_in(key, 1), (GROUPS, 1), 1, TOK_DEV // 2 + 1)
    second_cut = jax.random.randint(jax.random.fold_in(key, 2), (GROUPS, 1), TOK_DEV // 2 + 1, TOK_DEV)
    positions = jnp.arange(TOK_DEV, dtype=jnp.int32)[None, :]
    frames = (positions >= first_cut).astype(jnp.int32) + (positions >= second_cut).astype(jnp.int32)
    return frames.reshape(TOKENS)


def draw_reach(key, part):
    key = jax.random.fold_in(key, 53)
    offsets = jax.random.randint(key, (GROUPS,), 1, LAGS + 1)
    group_ids = jnp.arange(GROUPS, dtype=jnp.int32)
    limited = jnp.minimum(offsets, group_ids)
    limited = jnp.where(group_ids == 1, 0, limited)
    return jnp.where(group_ids == GROUPS - 1, LAGS, limited).astype(jnp.int32)


def level_of(stream_key, shape, pieces, smallest, largest):
    def one(position, parts):
        draws = jax.random.uniform(jax.random.fold_in(jax.random.fold_in(stream_key, 6), position), (parts,), jnp.float32, smallest / len(pieces), largest / len(pieces))
        return jnp.repeat(jnp.exp(draws), shape[position] // parts).reshape((-1,) + (1,) * (len(shape) - position - 1))

    loudness = one(*pieces[0])
    for cut in pieces[1:]:
        loudness = loudness * one(*cut)
    return loudness


def noise(key, extent, scale, bound, split=(), held_as=jnp.bfloat16):
    entries = jax.random.normal(key, extent, jnp.float32) * scale
    if len(split) > 0:
        entries = level_of(key, extent, split, -0.22, 0.18) * entries
    return jnp.clip(entries, min=-bound, max=bound).astype(held_as)


def setup_inputs(seed: int = 0) -> dict:
    key_list = jax.random.split(jax.random.key(seed), 9)
    q_raw = draw_q_raw(jax.random.fold_in(key_list[8], 71), 0)
    k_raw = draw_k_raw(jax.random.fold_in(key_list[8], 71), 0)
    v_in = draw_v_in(jax.random.fold_in(key_list[8], 71), 0)
    gain_q = jnp.clip(1.0 + 0.1 * jax.random.normal(key_list[3], (D,), jnp.float32), 0.5, 1.5)
    gain_k = jnp.clip(1.0 + 0.1 * jax.random.normal(key_list[4], (D,), jnp.float32), 0.5, 1.5)
    frame_index = draw_frame_index(jax.random.fold_in(key_list[8], 71), 0)
    reach = draw_reach(jax.random.fold_in(key_list[8], 71), 0)
    cotangent = noise(key_list[7], (TOKENS, D), 1.0, 6.0, ((0, 64), (1, 4)))
    return dict(q_raw=q_raw, k_raw=k_raw, v_in=v_in, gain_q=gain_q, gain_k=gain_k, frame_index=frame_index, reach=reach, cotangent=cotangent)


EPSILON = 1e-06

def narrowed(values):
    return lax.optimization_barrier(values.astype(jnp.bfloat16)).astype(jnp.float32)

def normalize(raw_rows, gain_row):
    values = raw_rows.astype(jnp.float32)
    row_rates = lax.rsqrt(lax.optimization_barrier(jnp.sum(values * values, axis=1)) / D + EPSILON)
    normed = (values * row_rates[:, None] * gain_row[None, :]).astype(jnp.bfloat16)
    return (normed, values, row_rates)

def norm_backward(grad_norm, values, row_rates, gain_row):
    gain_grad = lax.optimization_barrier(jnp.sum(grad_norm * values * row_rates[:, None], axis=0))
    inner_sum = lax.optimization_barrier(jnp.sum(gain_row[None, :] * grad_norm * values, axis=1))
    cubed = row_rates * row_rates * row_rates
    grad_raw = row_rates[:, None] * gain_row[None, :] * grad_norm - values * (cubed * inner_sum / D)[:, None]
    return (grad_raw.astype(jnp.bfloat16), gain_grad)

def key_sources(group_id, frame_index, reach):
    own_frames = lax.dynamic_slice_in_dim(frame_index, group_id * TOK_DEV, TOK_DEV)
    sources = [group_id]
    allowed = [(own_frames[None, :] <= own_frames[:, None])[None]]
    for offset in range(1, LAGS + 1):
        sources.append(jnp.maximum(group_id - offset, 0).astype(jnp.int32))
        allowed.append(offset <= reach[group_id])
    sources.append(jnp.zeros_like(group_id))
    allowed.append(group_id > reach[group_id])
    return (sources, allowed)

def block_scores(query_rows, key_rows, allowed_now):
    scores = jnp.einsum('thd,shd->hts', query_rows.astype(jnp.float32), key_rows.astype(jnp.float32)) * HD ** (-0.5)
    return jnp.where(allowed_now, scores, -jnp.inf)

def reference(q_raw, k_raw, v_in, gain_q, gain_k, frame_index, reach, cotangent):
    q_norm, q_vals, rate_q = normalize(q_raw, gain_q)
    k_norm, k_vals, rate_k = normalize(k_raw, gain_k)
    full_shape = (GROUPS, TOK_DEV, HEADS, HD)
    query_heads = q_norm.reshape(full_shape)
    key_heads = k_norm.reshape(full_shape)
    value_heads = v_in.reshape(full_shape)

    def forward_group(group_id):
        sources, allowed = key_sources(group_id, frame_index, reach)
        query_rows = query_heads[group_id]
        score_list = [block_scores(query_rows, key_heads[source], allowed_now) for source, allowed_now in zip(sources, allowed)]
        highest = reduce(jnp.maximum, [lax.optimization_barrier(jnp.max(scores_now, axis=2)) for scores_now in score_list])
        row_totals = jnp.zeros_like(highest)
        accumulated = jnp.zeros((TOK_DEV, HEADS, HD), jnp.float32)
        for scores_now, source in zip(score_list, sources):
            weights = jnp.exp(scores_now - highest[:, :, None])
            row_totals = row_totals + lax.optimization_barrier(jnp.sum(weights, axis=2))
            accumulated = accumulated + jnp.einsum('hts,shd->thd', narrowed(weights), value_heads[source].astype(jnp.float32))
        attn_rows = (accumulated / jnp.transpose(row_totals)[:, :, None]).astype(jnp.bfloat16)
        return (attn_rows, highest, row_totals)
    attn_blocks, block_tops, block_totals = lax.map(forward_group, jnp.arange(GROUPS, dtype=jnp.int32))
    attn_out = attn_blocks.reshape(TOKENS, D)
    chan_max = lax.optimization_barrier(jnp.max(jnp.abs(attn_out.astype(jnp.float32)), axis=0))
    scaled_out = (attn_out.astype(jnp.float32) / (chan_max + EPSILON)).astype(jnp.bfloat16)
    grad_attn = (cotangent.astype(jnp.float32) / (chan_max + EPSILON)).astype(jnp.bfloat16).reshape(full_shape)

    def backward_group(carry, group_id):
        key_grads, value_grads = carry
        sources, allowed = key_sources(group_id, frame_index, reach)
        query_rows = query_heads[group_id]
        query_wide = query_rows.astype(jnp.float32)
        grad_rows = grad_attn[group_id].astype(jnp.float32)
        row_delta = jnp.einsum('thd,thd->ht', grad_rows, attn_blocks[group_id].astype(jnp.float32))
        highest = block_tops[group_id]
        row_totals = block_totals[group_id]
        grad_query = jnp.zeros((TOK_DEV, HEADS, HD), jnp.float32)
        for source, allowed_now in zip(sources, allowed):
            scores_now = block_scores(query_rows, key_heads[source], allowed_now)
            attn_probs = jnp.exp(scores_now - highest[:, :, None]) / row_totals[:, :, None]
            grad_value = jnp.einsum('hts,thd->shd', narrowed(attn_probs), grad_rows)
            grad_prob = jnp.einsum('thd,shd->hts', grad_rows, value_heads[source].astype(jnp.float32))
            grad_score = narrowed(attn_probs * (grad_prob - row_delta[:, :, None]))
            grad_query = grad_query + jnp.einsum('hts,shd->thd', grad_score, key_heads[source].astype(jnp.float32)) * HD ** (-0.5)
            grad_key = jnp.einsum('hts,thd->shd', grad_score, query_wide) * HD ** (-0.5)
            key_grads = key_grads.at[source].add(grad_key)
            value_grads = value_grads.at[source].add(grad_value)
        return ((key_grads, value_grads), grad_query)
    zero_grads = jnp.zeros(full_shape, jnp.float32)
    (key_grads, value_grads), grad_queries = lax.scan(backward_group, (zero_grads, zero_grads), jnp.arange(GROUPS, dtype=jnp.int32))
    grad_qn = grad_queries.reshape(TOKENS, D)
    grad_kn = key_grads.reshape(TOKENS, D)
    grad_v = value_grads.reshape(TOKENS, D).astype(jnp.bfloat16)
    grad_q, grad_gain_q = norm_backward(grad_qn, q_vals, rate_q, gain_q)
    grad_k, grad_gain_k = norm_backward(grad_kn, k_vals, rate_k, gain_k)
    return (scaled_out, grad_q, grad_k, grad_v, grad_gain_q, grad_gain_k)
```

```python
import jax
import jax.numpy as jnp
from jax import lax
from jax.experimental import pallas as pl
from jax.experimental.pallas import tpu as pltpu
from jax.sharding import PartitionSpec as P

D = 5120
HD = 128
XS = 4
ZS = 8
TOK = 128
HALF = 640
HEADS = HALF // HD
KEYS = 6 * TOK
QUARTER = TOK // XS
EPSILON = 1e-06
HIDDEN = -1e30
F32 = jnp.float32
BF16 = jnp.bfloat16


def chip_pairs(move):
    pairs = []
    for x in range(XS):
        for z in range(ZS):
            to = move(x, z)
            if to is not None:
                for core in range(2):
                    pairs.append(((x * ZS + z) * 2 + core, (to[0] * ZS + to[1]) * 2 + core))
    return pairs


def move_chips(value, move):
    return lax.ppermute(value, "frame", chip_pairs(move))


def line_shift(by):
    def move(x, z):
        chip = x * ZS + z + by
        return divmod(chip, ZS) if 0 <= chip < XS * ZS else None

    return move


def shift_x(value, by):
    return move_chips(value, lambda x, z: ((x + by) % XS, z))


def shift_z(value, by):
    return move_chips(value, lambda x, z: (x, (z + by) % ZS))


def swap_z(value, bit):
    return move_chips(value, lambda x, z: (x, z ^ bit))


def other_core(value):
    return lax.ppermute(value, "frame", [(i, i ^ 1) for i in range(2 * XS * ZS)])


def sum_heads(value):
    turns = [lax.ppermute(value, "head", [(i, (i + by) % 4) for i in range(4)]) for by in (2, 1, 3)]
    return (value + turns[0]) + (turns[1] + turns[2])


def pairs_of(turn):
    return lambda x, z: turn.get((x, z))


def column(moves, xs):
    return {(x, a): (x, b) for x in xs for a, b in moves.items()}


def row(a, b, zs):
    return {(a, z): (b, z) for z in zs}


SCATTER_X = tuple(row(0, to, (0,)) for to in range(1, XS))
GATHER_X = tuple(row(src, 0, (0,)) for src in range(1, XS))
SPREAD_Z = (
    (column({0: 3}, range(XS)), column({0: 5}, range(XS))),
    (column({0: 1, 3: 4, 5: 6}, range(XS)), column({0: 7, 3: 2}, range(XS))),
)
GATHER_Z = (
    (column({1: 0, 4: 3, 6: 5}, range(XS)), column({7: 0, 2: 3}, range(XS))),
    (column({3: 0}, range(XS)), column({5: 0}, range(XS))),
)


def spread_sink(quarters, root):
    total = jnp.where(root, quarters[0], jnp.zeros_like(quarters[0]))
    for quarter, turn in zip(quarters[1:], SCATTER_X):
        total = total + move_chips(quarter, pairs_of(turn))
    for turns in SPREAD_Z:
        got = [move_chips(total, pairs_of(turn)) for turn in turns]
        total = total + got[0] + got[1]
    return [total] + [shift_x(total, by) for by in (1, 2, 3)]


def gather_z(total, index):
    low = total.astype(BF16)
    got = [move_chips(low, pairs_of(turn)) for turn in GATHER_Z[index]]
    return total + got[0].astype(F32) + got[1].astype(F32)


def after(values, *others):
    return lax.optimization_barrier((values, others))[0]


def pairs_z(value, join):
    return join(value, swap_z(value, 1))


def quads_z(value, join):
    turns = [shift_z(value, by) for by in (4, 2, 6)]
    return join(join(value, turns[0]), join(turns[1], turns[2]))


def quads_x(value, join):
    turns = [shift_x(value, by) for by in (2, 1, 3)]
    return join(join(value, turns[0]), join(turns[1], turns[2]))


def contract(a, b, dims, **kw):
    return lax.dot_general(a, b, (dims, ((), ())), preferred_element_type=F32, **kw)


def lane_sums(block):
    ones = jnp.ones((8, HD), F32)
    return contract(ones, block, ((1,), (1,)), precision=lax.Precision.HIGHEST)[:1]


def upright(line):
    return jnp.broadcast_to(line, (TOK, TOK)).T[:, :1]


def fold(block):
    total = block[:, :HD]
    for start in range(HD, block.shape[1], HD):
        total = total + block[:, start : start + HD]
    return total


def sums_kernel(q, k, sums):
    for row, ref in enumerate((q, k)):
        values = ref[...].astype(F32)
        sums[row : row + 1] = lane_sums(fold(values * values))


def split_kernel(core, q, k, v, c, keep, send):
    mine = pl.ds(pl.multiple_of(core[0] * HALF, HD), HALF)
    other = pl.ds(pl.multiple_of((1 - core[0]) * HALF, HD), HALF)
    for index, ref in enumerate((q, k, v, c)):
        keep[index] = ref[:, mine]
        send[index] = ref[:, other]


def norm_kernel(place, keep, got, tags, tags_got, gain_q, gain_k, q_norm, k_norm, bias, *quarters):
    for half, (source, tag) in enumerate(((keep, tags), (got, tags_got))):
        rows = slice(half * TOK, (half + 1) * TOK)
        rate_q = upright(lax.rsqrt(tag[0:1] / D + EPSILON))
        rate_k = upright(lax.rsqrt(tag[1:2] / D + EPSILON))
        q_norm[rows] = (source[0].astype(F32) * rate_q * gain_q[...]).astype(BF16)
        k_norm[rows] = (source[1].astype(F32) * rate_k * gain_k[...]).astype(BF16)
    core = place[0] % 2

    def fill(source, start):
        for index, quarter in enumerate(quarters):
            quarter[:, :HALF] = k_norm[start + index * QUARTER : start + (index + 1) * QUARTER]
            quarter[:, HALF:] = source[2, index * QUARTER : (index + 1) * QUARTER]

    @pl.when(core == 0)
    def _():
        fill(keep, 0)

    @pl.when(core == 1)
    def _():
        fill(got, TOK)

    chip = place[0] // 2
    groups = (place[0], place[0] + 1 - 2 * core)
    ahead = 2 * chip - 2 + core
    key_groups = groups + (ahead, 4 * chip - 3 - ahead, 2 * chip - 3)
    nothing = jnp.zeros((TOK, TOK), F32)
    for half, tag in enumerate((tags, tags_got)):
        rows = slice(half * TOK, (half + 1) * TOK)
        frames = tag[2:3]
        reach = jnp.broadcast_to(tag[3:4], (TOK, TOK))
        for block in range(6):
            cols = slice(block * TOK, (block + 1) * TOK)
            if block == half:
                seen = frames <= upright(frames)
            elif block == 5:
                seen = reach < (nothing + groups[half].astype(F32))
            else:
                back = nothing + (groups[half] - key_groups[block]).astype(F32)
                seen = (back >= 1.0) & (back <= reach)
            bias[rows, cols] = jnp.where(seen, 0.0, HIDDEN)


def lanes_of(head):
    return slice(head * HD, (head + 1) * HD)


def key_rows(blocks, lanes):
    return jnp.concatenate([ref[:, lanes] for ref in blocks], axis=0)


def forward_kernel(
    place, bias, q, ko, kp, ke, vo, vp, ve, s0, s1, s2, s3, attn, top, probs, sink
):
    x = place[0] // (2 * ZS)
    for by, part in enumerate((s0, s1, s2, s3)):
        start = pl.multiple_of(((x + XS - by) % XS) * QUARTER, QUARTER)
        sink[pl.ds(start, QUARTER)] = part[...]
    for head in range(HEADS):
        lanes = lanes_of(head)
        keys = jnp.concatenate([key_rows((ko, kp, ke), lanes), sink[:, lanes]], axis=0)
        values = jnp.concatenate(
            [key_rows((vo, vp, ve), lanes), sink[:, lanes_of(HEADS + head)]], axis=0
        )
        scores = contract(q[:, lanes], keys, ((1,), (1,))) * HD ** (-0.5) + bias[...]
        highest = jnp.max(scores, axis=1, keepdims=True)
        weights = jnp.exp(scores - highest)
        total = jnp.sum(weights, axis=1, keepdims=True)
        inverse = 1.0 / total
        summed = contract(weights.astype(BF16), values, ((1,), (0,)))
        rows = (summed * inverse).astype(BF16)
        attn[:, lanes] = rows
        top[:, lanes] = jnp.max(jnp.abs(rows.astype(F32)), axis=0, keepdims=True)
        probs[head] = (weights * inverse).astype(BF16)


def value_kernel(probs, keep, got, own, prev, early, sink):
    for head in range(HEADS):
        lanes = lanes_of(head)
        cot = jnp.concatenate([keep[3, :, lanes], got[3, :, lanes]], axis=0)
        grads = contract(probs[head], cot, ((0,), (0,)))
        own[:, lanes] = grads[: 2 * TOK]
        prev[:, lanes] = grads[2 * TOK : 4 * TOK].astype(BF16)
        early[:, lanes] = grads[4 * TOK : 5 * TOK].astype(BF16)
        sink[:, lanes] = grads[5 * TOK :].astype(BF16)


def sink_kernel(
    place, probs, keep, got, attn, chan, q, sink, v_low, p0, p1, p2, p3, grad_attn, delta, scaled, rows
):
    for head in range(HEADS):
        lanes = lanes_of(head)
        scale = chan[:, lanes] + EPSILON
        cot = jnp.concatenate([keep[3, :, lanes], got[3, :, lanes]], axis=0).astype(F32)
        grads = (cot / scale).astype(BF16)
        grad_attn[:, lanes] = grads
        out = attn[:, lanes].astype(F32)
        scaled[:, lanes] = (out / scale).astype(BF16)
        sums = jnp.sum(grads.astype(F32) * out, axis=1, keepdims=True)
        delta[:, lanes] = jnp.broadcast_to(sums, (2 * TOK, HD))
        grad_prob = contract(grads, sink[:, lanes_of(HEADS + head)], ((1,), (1,)))
        grad_score = (probs[head, :, 5 * TOK :].astype(F32) * (grad_prob - sums)).astype(BF16)
        rows[:, lanes] = contract(grad_score, q[:, lanes], ((0,), (0,))) * HD ** (-0.5)
    x = place[0] // (2 * ZS)
    for by, part in enumerate((p0, p1, p2, p3)):
        take = pl.ds(pl.multiple_of(((x + by) % XS) * QUARTER, QUARTER), QUARTER)
        part[:, :HALF] = rows[take].astype(BF16)
        part[:, HALF:] = v_low[take]


def backward_kernel(
    probs, grad_attn, delta, q, ko, kp, ke, vo, vp, ve, sink,
    grad_q, own, prev, early, gain_sum, inner,
):
    inner_q = jnp.zeros((2 * TOK, HD), F32)
    inner_k = jnp.zeros((KEYS, HD), F32)
    for head in range(HEADS):
        lanes = lanes_of(head)
        keys = jnp.concatenate([key_rows((ko, kp, ke), lanes), sink[:, lanes]], axis=0)
        values = jnp.concatenate(
            [key_rows((vo, vp, ve), lanes), sink[:, lanes_of(HEADS + head)]], axis=0
        )
        query = q[:, lanes]
        grad_prob = contract(grad_attn[:, lanes], values, ((1,), (1,)))
        row_delta = jnp.concatenate([delta[:, lanes]] * 6, axis=1)
        grad_score = (probs[head].astype(F32) * (grad_prob - row_delta)).astype(BF16)
        rows = contract(grad_score, keys, ((1,), (0,))) * HD ** (-0.5)
        grad_q[:, lanes] = rows
        product = rows * query.astype(F32)
        gain_sum[:, lanes] = jnp.sum(product, axis=0, keepdims=True)
        inner_q = inner_q + product
        grads = contract(grad_score, query, ((0,), (0,))) * HD ** (-0.5)
        inner_k = inner_k + grads * keys.astype(F32)
        own[:, lanes] = grads[: 2 * TOK]
        prev[:, lanes] = grads[2 * TOK : 4 * TOK].astype(BF16)
        early[:, lanes] = grads[4 * TOK : 5 * TOK].astype(BF16)
    for block in range(2):
        inner[block : block + 1] = lane_sums(inner_q[block * TOK : (block + 1) * TOK])
    for block in range(6):
        inner[block + 2 : block + 3] = lane_sums(inner_k[block * TOK : (block + 1) * TOK])


def pack_kernel(k_prev, k_early, inner, near, far):
    near[:, :HALF] = k_prev[...]
    far[:, :HALF] = k_early[...]
    lane = lax.broadcasted_iota(jnp.int32, (TOK, HD), 1)
    for block in range(3):
        tall = jnp.broadcast_to(inner[4 + block : 5 + block], (TOK, TOK)).T
        whole = tall.astype(BF16).astype(F32)
        both = jnp.where(lane == 0, whole, tall - whole).astype(BF16)
        if block < 2:
            near[block * TOK : (block + 1) * TOK, HALF:] = both
        else:
            far[:, HALF:] = both


def finish(grad, raw, rate, gains, inner):
    return (rate * gains * grad - raw.astype(F32) * (rate * rate * inner / D)).astype(BF16)


def query_kernel(grad, keep, got, tags, tags_got, gain_q, inner, mine, other):
    for half, (source, tag, out) in enumerate(((keep, tags, mine), (got, tags_got, other))):
        rows = slice(half * TOK, (half + 1) * TOK)
        rate = upright(lax.rsqrt(tag[0:1] / D + EPSILON))
        sums = upright(inner[half : half + 1])
        out[...] = finish(grad[rows], source[0], rate, gain_q[...], sums)


def key_kernel(
    place, k_own, v_own, near, far, v_near, v_far, s0, s1, s2, s3, inner, sink_inner, chan,
    keep, got, tags, tags_got, gain_k, mine, other,
):
    sunk = jnp.concatenate([ref[...].astype(F32) for ref in (s0, s1, s2, s3)], axis=0)
    core = place[0] % 2
    scale = chan[...] + EPSILON
    for half, (source, tag, out) in enumerate(((keep, tags, mine), (got, tags_got, other))):
        rows = slice(half * TOK, (half + 1) * TOK)
        use_far = jnp.where((core + half) == 1, 1.0, 0.0)
        use_sink = jnp.where(place[0] < 2, 1.0, 0.0) * (1.0 - use_far)
        rate = upright(lax.rsqrt(tag[1:2] / D + EPSILON))
        grad = k_own[rows] + near[rows, :HALF].astype(F32)
        grad = grad + use_far * far[:, :HALF].astype(F32) + use_sink * sunk[:, :HALF]
        sums = upright(inner[2 + half : 3 + half] + use_sink * sink_inner[...])
        extra = near[rows, HALF:].astype(F32) + use_far * far[:, HALF:].astype(F32)
        sums = sums + extra[:, 0:1] + extra[:, 1:2]
        out[0] = finish(grad, source[1], rate, gain_k[...], sums)
        grad = v_own[rows] + v_near[rows].astype(F32)
        grad = grad + use_far * v_far[...].astype(F32) + use_sink * sunk[:, HALF:]
        out[1] = (grad / scale).astype(BF16)


def shape(*dims, kind=F32):
    return jax.ShapeDtypeStruct(dims, kind)


def call(kernel, outs, flops=0, moved=2 * 1024 * 1024, exps=0, scalar=False, args=0):
    more = {}
    if scalar:
        more["in_specs"] = [pl.BlockSpec(memory_space=pltpu.SMEM)] + [
            pl.BlockSpec(memory_space=pltpu.VMEM)
        ] * args
    return pl.pallas_call(
        kernel,
        out_shape=outs,
        compiler_params=pltpu.CompilerParams(vmem_limit_bytes=48 * 1024 * 1024),
        cost_estimate=pl.CostEstimate(flops=flops, bytes_accessed=moved, transcendentals=exps),
        **more,
    )


def per_device(q_raw, k_raw, v_in, gain_q, gain_k, frame_index, reach, cotangent):
    place = lax.axis_index("frame")
    places = place.reshape(1)
    core = place % 2
    first = core == 0
    root = place < 2
    block_flops = 2 * 2 * TOK * KEYS * HALF
    low_half = lambda rows: shape(rows, HALF, kind=BF16)
    sums = call(sums_kernel, shape(2, TOK), moved=700000)(q_raw, k_raw)
    totals = sum_heads(sums)
    keep, send = call(
        split_kernel, (shape(4, TOK, HALF, kind=BF16),) * 2, scalar=True, args=4
    )(core.reshape(1), q_raw, k_raw, v_in, cotangent)
    got = other_core(send)
    second_group = lambda both: jnp.where(first, both[TOK:], both[:TOK])
    v2 = jnp.concatenate([keep[2], got[2]], axis=0)
    v_prev = move_chips(v2, line_shift(1))
    v_early = move_chips(second_group(v_prev), line_shift(1))
    tags = jnp.concatenate(
        [totals, frame_index.astype(F32)[None], jnp.broadcast_to(reach.astype(F32), (1, TOK))]
    )
    tags_got = other_core(tags)
    pick = lambda value: jnp.where(first, value[:HALF], value[HALF:])[None, :]
    gains_q, gains_k = pick(gain_q), pick(gain_k)
    quarter = shape(QUARTER, 2 * HALF, kind=BF16)
    q_norm, k_norm, bias, *quarters = call(
        norm_kernel,
        (low_half(2 * TOK), low_half(2 * TOK), shape(2 * TOK, KEYS)) + (quarter,) * XS,
        scalar=True,
        args=6,
    )(places, keep, got, tags, tags_got, gains_q, gains_k)
    k_prev_in = move_chips(k_norm, line_shift(1))
    k_early_in = move_chips(second_group(k_prev_in), line_shift(1))
    parts = spread_sink(quarters, root)
    blocks = (k_norm, k_prev_in, k_early_in, v2, v_prev, v_early)

    attn, top, probs, sink = call(
        forward_kernel,
        (
            low_half(2 * TOK),
            shape(1, HALF),
            shape(HEADS, 2 * TOK, KEYS, kind=BF16),
            shape(TOK, 2 * HALF, kind=BF16),
        ),
        2 * block_flops,
        6 * 1024 * 1024,
        HEADS * 2 * TOK * KEYS,
        scalar=True,
        args=12,
    )(places, bias, q_norm, *blocks, *parts)

    pair = pairs_z(top, jnp.maximum)
    v_own, v_prev_out, v_early_out, v_low = call(
        value_kernel,
        (shape(2 * TOK, HALF), low_half(2 * TOK), low_half(TOK), low_half(TOK)),
        block_flops,
        4 * 1024 * 1024,
    )(probs, keep, got)
    pair, v_low, v_prev_out, v_early_out = after((pair, v_low, v_prev_out, v_early_out))
    v_near = move_chips(v_prev_out, line_shift(-1))
    v_far = move_chips(v_early_out, line_shift(-2))
    quad = quads_z(pair, jnp.maximum)
    chan = quads_x(quad, jnp.maximum)
    chan, v_near, v_far = after((chan, v_near, v_far))

    *pieces, grad_attn, delta, scaled = pl.pallas_call(
        sink_kernel,
        out_shape=(quarter,) * XS
        + (low_half(2 * TOK), shape(2 * TOK, HALF), low_half(2 * TOK)),
        in_specs=[pl.BlockSpec(memory_space=pltpu.SMEM)]
        + [pl.BlockSpec(memory_space=pltpu.VMEM)] * 8,
        scratch_shapes=[pltpu.VMEM((TOK, HALF), F32)],
        compiler_params=pltpu.CompilerParams(vmem_limit_bytes=48 * 1024 * 1024),
        cost_estimate=pl.CostEstimate(
            flops=block_flops // 3, bytes_accessed=4 * 1024 * 1024, transcendentals=0
        ),
    )(places, probs, keep, got, attn, chan, q_norm, sink, v_low)
    total = pieces[0].astype(F32)
    for by in (1, 2, 3):
        total = total + shift_x(pieces[by], by).astype(F32)
    grad_qn, k_own, k_prev, k_early, gain_sum, inner = call(
        backward_kernel,
        (
            shape(2 * TOK, HALF),
            shape(2 * TOK, HALF),
            low_half(2 * TOK),
            low_half(TOK),
            shape(1, HALF),
            shape(8, TOK),
        ),
        3 * block_flops,
        8 * 1024 * 1024,
    )(probs, grad_attn, delta, q_norm, *blocks, sink)
    inner_got = other_core(inner)
    inner = inner + inner_got[jnp.array([1, 0, 3, 2, 5, 4, 6, 7])]

    inner, total = after((inner, total))
    total = gather_z(total, 0)
    inner = sum_heads(inner)
    near, far = call(
        pack_kernel, (shape(2 * TOK, HALF + HD, kind=BF16), shape(TOK, HALF + HD, kind=BF16))
    )(k_prev, k_early, inner)
    sums = jnp.concatenate([gain_sum.reshape(HEADS, HD), inner[7:8]])

    sums, total, near, far = after((sums, total, near, far))
    near_got = move_chips(near, line_shift(-1))
    total = gather_z(total, 1)
    sums = pairs_z(sums, jnp.add)
    sums, total, far = after((sums, total, far))
    far_got = move_chips(far, line_shift(-2))
    low = total.astype(BF16)
    sunk = [total] + [move_chips(low, pairs_of(turn)) for turn in GATHER_X]
    sums = quads_z(sums, jnp.add)
    sums, sunk, near_got, far_got = after((sums, sunk, near_got, far_got))
    sums = quads_x(sums, jnp.add)

    q_mine, q_other = call(query_kernel, (low_half(TOK), low_half(TOK)))(
        grad_qn, keep, got, tags, tags_got, gains_q, inner
    )
    both = shape(2, TOK, HALF, kind=BF16)
    mine, other = call(key_kernel, (both, both), scalar=True, args=18)(
        places, k_own, v_own, near_got, far_got, v_near, v_far, *sunk, inner, sums[HEADS:], chan,
        keep, got, tags, tags_got, gains_k,
    )

    def cores_out(mine, other):
        theirs = other_core(other)
        return jnp.where(
            first,
            jnp.concatenate([mine, theirs], axis=-1),
            jnp.concatenate([theirs, mine], axis=-1),
        )

    scaled_out = cores_out(scaled[:TOK], scaled[TOK:])
    grad_q = cores_out(q_mine, q_other)
    theirs = other_core(other)
    join = lambda a, b: jnp.where(
        first, jnp.concatenate([a, b], axis=1), jnp.concatenate([b, a], axis=1)
    )
    grad_k = join(mine[0], theirs[0])
    grad_v = join(mine[1], theirs[1])
    gain_total = sums[:HEADS].reshape(1, HALF)
    gain_both = cores_out(gain_total, gain_total)[0]
    return (scaled_out, grad_q, grad_k, grad_v, gain_both / gain_q, gain_both / gain_k)


def solution(mesh):
    rows = P("frame", "head")
    placed = (rows, rows, rows, P("head"), P("head"), P("frame"), P("frame"), rows)
    return jax.shard_map(
        per_device,
        mesh=mesh,
        in_specs=placed,
        out_specs=(rows, rows, rows, rows, P("head"), P("head")),
        check_vma=False,
    )
```

```python
import jax
import jax.numpy as jnp
from jax import lax
from jax.experimental import pallas as pl
from jax.experimental.pallas import tpu as pltpu
from jax.sharding import PartitionSpec as P

D = 5120
HD = 128
XS = 4
ZS = 8
TOK = 128
HALF = 640
HEADS = HALF // HD
KEYS = 6 * TOK
QUARTER = TOK // XS
CUTS = 2
EPSILON = 1e-06
HIDDEN = -1e30
F32 = jnp.float32
BF16 = jnp.bfloat16


def chip_pairs(move):
    pairs = []
    for x in range(XS):
        for z in range(ZS):
            to = move(x, z)
            if to is not None:
                for core in range(2):
                    pairs.append(((x * ZS + z) * 2 + core, (to[0] * ZS + to[1]) * 2 + core))
    return pairs


def move_chips(value, move):
    return lax.ppermute(value, "frame", chip_pairs(move))


def line_shift(by):
    def move(x, z):
        chip = x * ZS + z + by
        return divmod(chip, ZS) if 0 <= chip < XS * ZS else None

    return move


def shift_x(value, by):
    return move_chips(value, lambda x, z: ((x + by) % XS, z))


def shift_z(value, by):
    return move_chips(value, lambda x, z: (x, (z + by) % ZS))


def swap_z(value, bit):
    return move_chips(value, lambda x, z: (x, z ^ bit))


def other_core(value):
    return lax.ppermute(value, "frame", [(i, i ^ 1) for i in range(2 * XS * ZS)])


def head_turns(value):
    return [lax.ppermute(value, "head", [(i, (i + by) % 4) for i in range(4)]) for by in (2, 1, 3)]


def sum_heads(value):
    turns = head_turns(value)
    return (value + turns[0]) + (turns[1] + turns[2])


def pairs_of(turn):
    return lambda x, z: turn.get((x, z))


def column(moves, xs):
    return {(x, a): (x, b) for x in xs for a, b in moves.items()}


def row(a, b, zs):
    return {(a, z): (b, z) for z in zs}


SCATTER_X = tuple(row(0, to, (0,)) for to in range(1, XS))
GATHER_X = tuple(row(src, 0, range(ZS)) for src in (2, 1, 3))
SPREAD_Z = (
    (column({0: 5}, range(XS)), column({0: 6}, range(XS))),
    (column({0: 7, 5: 3, 6: 4}, range(XS)), column({0: 1, 5: 2}, range(XS))),
)
GATHER_Z = (
    (column({1: 0, 4: 3, 6: 5}, (0,)), column({7: 0, 2: 3}, (0,))),
    (column({3: 0}, (0,)), column({5: 0}, (0,))),
)


def add_parts(*parts, moved=0):
    first = parts[0]
    return call(
        add_kernel,
        jax.ShapeDtypeStruct(first.shape, BF16),
        moved=moved or 2 * (len(parts) + 1) * first.size,
    )(*parts)


def rounds(turns, low):
    return [move_chips(low, pairs_of(turn)) for turn in turns]


def after(values, *others):
    return lax.optimization_barrier((values, others))[0]


def pairs_z(value, join):
    return join(value, swap_z(value, 1))


def quads_z(value, join):
    turns = [shift_z(value, by) for by in (4, 2, 6)]
    return join(join(value, turns[0]), join(turns[1], turns[2]))


def quads_x(value, join):
    turns = [shift_x(value, by) for by in (2, 1, 3)]
    return join(join(value, turns[0]), join(turns[1], turns[2]))


def contract(a, b, dims, **kw):
    return lax.dot_general(a, b, (dims, ((), ())), preferred_element_type=F32, **kw)


def lane_sums(block):
    ones = jnp.ones((8, HD), F32)
    return contract(ones, block, ((1,), (1,)), precision=lax.Precision.HIGHEST)[:1]


def upright(line):
    return jnp.broadcast_to(line, (TOK, TOK)).T[:, :1]


def fold(block):
    total = block[:, :HD]
    for start in range(HD, block.shape[1], HD):
        total = total + block[:, start : start + HD]
    return total


def entry_kernel(core, q, k, v, c, keep, send, sums, held, sems):
    step = TOK // CUTS
    copies = []
    for index, ref in enumerate((q, k, v, c)):
        for cut in range(CUTS):
            rows = pl.ds(cut * step, step)
            copies.append(
                pltpu.make_async_copy(ref.at[rows], held.at[index, rows], sems.at[index, cut])
            )
    for copy in copies:
        copy.start()
    mine = pl.ds(pl.multiple_of(core[0] * HALF, HD), HALF)
    other = pl.ds(pl.multiple_of((1 - core[0]) * HALF, HD), HALF)
    for index in range(4):
        for copy in copies[index * CUTS : (index + 1) * CUTS]:
            copy.wait()
        keep[index] = held[index, :, mine]
        send[index] = held[index, :, other]
        if index < 2:
            values = held[index].astype(F32)
            sums[index : index + 1] = lane_sums(fold(values * values))


def add_kernel(*refs):
    value = refs[0][...].astype(F32)
    for part in refs[1:-1]:
        value = value + part[...].astype(F32)
    refs[-1][...] = value.astype(BF16)


def norm_kernel(place, keep, got, tags, tags_got, gain_q, gain_k, q_norm, k_norm, bias, *quarters):
    for half, (source, tag) in enumerate(((keep, tags), (got, tags_got))):
        rows = slice(half * TOK, (half + 1) * TOK)
        rate_q = upright(lax.rsqrt(tag[0:1] / D + EPSILON))
        rate_k = upright(lax.rsqrt(tag[1:2] / D + EPSILON))
        q_norm[rows] = (source[0].astype(F32) * rate_q * gain_q[...]).astype(BF16)
        k_norm[rows] = (source[1].astype(F32) * rate_k * gain_k[...]).astype(BF16)
    core = place[0] % 2

    def fill(source, start):
        for index, quarter in enumerate(quarters):
            rows = slice(index * QUARTER, (index + 1) * QUARTER)
            quarter[:, :HALF] = k_norm[start + rows.start : start + rows.stop]
            quarter[:, HALF:] = source[2, rows]

    @pl.when(core == 0)
    def _():
        fill(keep, 0)

    @pl.when(core == 1)
    def _():
        fill(got, TOK)

    @pl.when(place[0] >= 2)
    def _():
        quarters[0][...] = jnp.zeros((QUARTER, 2 * HALF), BF16)

    chip = place[0] // 2
    groups = (place[0], place[0] + 1 - 2 * core)
    ahead = 2 * chip - 2 + core
    key_groups = groups + (ahead, 4 * chip - 3 - ahead, 2 * chip - 3)
    nothing = jnp.zeros((TOK, TOK), F32)
    for half, tag in enumerate((tags, tags_got)):
        rows = slice(half * TOK, (half + 1) * TOK)
        frames = tag[2:3]
        reach = jnp.broadcast_to(tag[3:4], (TOK, TOK))
        for block in range(6):
            cols = slice(block * TOK, (block + 1) * TOK)
            if block == half:
                seen = frames <= upright(frames)
            elif block == 5:
                seen = reach < (nothing + groups[half].astype(F32))
            else:
                back = nothing + (groups[half] - key_groups[block]).astype(F32)
                seen = (back >= 1.0) & (back <= reach)
            bias[rows, cols] = jnp.where(seen, 0.0, HIDDEN)


def lanes_of(head):
    return slice(head * HD, (head + 1) * HD)


def key_rows(blocks, lanes):
    return jnp.concatenate([ref[:, lanes] for ref in blocks], axis=0)


def forward_kernel(
    place, bias, q, ko, kp, ke, vo, vp, ve, s0, s1, s2, s3, attn, top, probs, sink
):
    x = place[0] // (2 * ZS)
    for by, part in enumerate((s0, s1, s2, s3)):
        start = pl.multiple_of(((x + XS - by) % XS) * QUARTER, QUARTER)
        sink[pl.ds(start, QUARTER)] = part[...]
    for head in range(HEADS):
        lanes = lanes_of(head)
        keys = key_rows((ko, kp, ke, sink), lanes)
        values = jnp.concatenate(
            [key_rows((vo, vp, ve), lanes), sink[:, lanes_of(HEADS + head)]], axis=0
        )
        scores = contract(q[:, lanes], keys, ((1,), (1,))) * HD ** (-0.5) + bias[...]
        highest = jnp.max(scores, axis=1, keepdims=True)
        weights = jnp.exp(scores - highest)
        total = jnp.sum(weights, axis=1, keepdims=True)
        inverse = 1.0 / total
        summed = contract(weights.astype(BF16), values, ((1,), (0,)))
        rows = (summed * inverse).astype(BF16)
        attn[:, lanes] = rows
        top[:, lanes] = jnp.max(jnp.abs(rows.astype(F32)), axis=0, keepdims=True)
        probs[head] = (weights * inverse).astype(BF16)


def value_kernel(probs, keep, got, own, prev, early, sink):
    for head in range(HEADS):
        lanes = lanes_of(head)
        cot = jnp.concatenate([keep[3, :, lanes], got[3, :, lanes]], axis=0)
        grads = contract(probs[head], cot, ((0,), (0,)))
        own[:, lanes] = grads[: 2 * TOK]
        prev[:, lanes] = grads[2 * TOK : 4 * TOK].astype(BF16)
        early[:, lanes] = grads[4 * TOK : 5 * TOK].astype(BF16)
        sink[:, lanes] = grads[5 * TOK :].astype(BF16)


def backward_kernel(
    probs, keep, got, attn, chan, q, ko, kp, ke, vo, vp, ve, sink, v_low, v_early,
    low, grad_q, own, prev, early, scaled, gain_sum, inner,
):
    inner_q = jnp.zeros((2 * TOK, HD), F32)
    inner_sink = jnp.zeros((TOK, HD), F32)
    for head in range(HEADS):
        lanes = lanes_of(head)
        keys = jnp.concatenate([key_rows((ko, kp, ke), lanes), sink[:, lanes]], axis=0)
        values = jnp.concatenate(
            [key_rows((vo, vp, ve), lanes), sink[:, lanes_of(HEADS + head)]], axis=0
        )
        query = q[:, lanes]
        scale = chan[:, lanes] + EPSILON
        cot = jnp.concatenate([keep[3, :, lanes], got[3, :, lanes]], axis=0).astype(F32)
        grad_attn = (cot / scale).astype(BF16)
        out = attn[:, lanes].astype(F32)
        scaled[:, lanes] = (out / scale).astype(BF16)
        delta = jnp.sum(grad_attn.astype(F32) * out, axis=1, keepdims=True)
        grad_prob = contract(grad_attn, values, ((1,), (1,)))
        grad_score = (probs[head].astype(F32) * (grad_prob - delta)).astype(BF16)
        rows = contract(grad_score, keys, ((1,), (0,))) * HD ** (-0.5)
        grad_q[:, lanes] = rows
        product = rows * query.astype(F32)
        gain_sum[:, lanes] = jnp.sum(product, axis=0, keepdims=True)
        inner_q = inner_q + product
        grads = contract(grad_score, query, ((0,), (0,))) * HD ** (-0.5)
        inner_sink = inner_sink + grads[5 * TOK :] * keys[5 * TOK :].astype(F32)
        own[:, lanes] = grads[: 2 * TOK]
        prev[:, lanes] = grads[2 * TOK : 4 * TOK].astype(BF16)
        early[:, lanes] = grads[4 * TOK : 5 * TOK].astype(BF16)
        low[:, lanes] = grads[5 * TOK :].astype(BF16)
    low[:, HALF:] = v_low[...]
    early[:, HALF:] = v_early[...]
    inner[0:1] = lane_sums(inner_q[:TOK])
    inner[1:2] = lane_sums(inner_q[TOK:])
    inner[2:3] = lane_sums(inner_sink)


def key_sum_kernel(
    place, own, near, far, k_norm, inner, p0, p1, p2, p3, total, low, mine, other
):
    core = place[0] % 2
    rows = [inner[0:1], inner[1:2]]
    for half in range(2):
        part = slice(half * TOK, (half + 1) * TOK)
        use_far = jnp.where((core + half) == 1, 1.0, 0.0)
        grad = own[part] + near[part].astype(F32) + use_far * far[:, :HALF].astype(F32)
        total[part] = grad
        rows.append(lane_sums(fold(grad * k_norm[part].astype(F32))))
    parts = (p0[...].astype(F32) + p1[...].astype(F32)) + (
        p2[...].astype(F32) + p3[...].astype(F32)
    )
    low[...] = parts.astype(BF16)
    rows.append(inner[2:3])
    for row, there in enumerate((1, 0, 3, 2, 4)):
        mine[row : row + 1] = rows[row]
        other[there : there + 1] = rows[row]
    mine[5:8] = jnp.zeros((3, TOK), F32)
    other[5:8] = jnp.zeros((3, TOK), F32)


def finish(grad, raw, rate, gains, inner):
    return (rate * gains * grad - raw.astype(F32) * (rate * rate * inner / D)).astype(BF16)


def query_kernel(grad, keep, got, tags, tags_got, gain_q, inner, mine, other):
    for half, (source, tag, out) in enumerate(((keep, tags, mine), (got, tags_got, other))):
        rows = slice(half * TOK, (half + 1) * TOK)
        rate = upright(lax.rsqrt(tag[0:1] / D + EPSILON))
        sums = upright(inner[half : half + 1])
        out[...] = finish(grad[rows], source[0], rate, gain_q[...], sums)


def key_kernel(
    place, k_total, v_own, v_near, far, sunk, inner, sink_inner, chan,
    keep, got, tags, tags_got, gain_k, mine, other,
):
    core = place[0] % 2
    scale = chan[...] + EPSILON
    for half, (source, tag, out) in enumerate(((keep, tags, mine), (got, tags_got, other))):
        rows = slice(half * TOK, (half + 1) * TOK)
        use_far = jnp.where((core + half) == 1, 1.0, 0.0)
        use_sink = jnp.where(place[0] < 2, 1.0, 0.0) * (1.0 - use_far)
        rate = upright(lax.rsqrt(tag[1:2] / D + EPSILON))
        grad = k_total[rows] + use_sink * sunk[:, :HALF].astype(F32)
        sums = upright(inner[2 + half : 3 + half] + use_sink * sink_inner[...])
        out[0] = finish(grad, source[1], rate, gain_k[...], sums)
        grad = v_own[rows] + v_near[rows].astype(F32)
        grad = grad + use_far * far[:, HALF:].astype(F32) + use_sink * sunk[:, HALF:].astype(F32)
        out[1] = (grad / scale).astype(BF16)


def shape(*dims, kind=F32):
    return jax.ShapeDtypeStruct(dims, kind)


def call(kernel, outs, flops=0, moved=2 * 1024 * 1024, exps=0, scalar=False, args=0):
    more = {}
    if scalar:
        more["in_specs"] = [pl.BlockSpec(memory_space=pltpu.SMEM)] + [
            pl.BlockSpec(memory_space=pltpu.VMEM)
        ] * args
    return pl.pallas_call(
        kernel,
        out_shape=outs,
        compiler_params=pltpu.CompilerParams(vmem_limit_bytes=20 * 1024 * 1024),
        cost_estimate=pl.CostEstimate(flops=flops, bytes_accessed=moved, transcendentals=exps),
        **more,
    )


def per_device(q_raw, k_raw, v_in, gain_q, gain_k, frame_index, reach, cotangent):
    place = lax.axis_index("frame")
    places = place.reshape(1)
    core = place % 2
    first = core == 0
    root = place < 2
    block_flops = 2 * 2 * TOK * KEYS * HALF
    low_half = lambda rows: shape(rows, HALF, kind=BF16)
    keep, send, sums = pl.pallas_call(
        entry_kernel,
        out_shape=(shape(4, TOK, HALF, kind=BF16),) * 2 + (shape(2, TOK),),
        in_specs=[pl.BlockSpec(memory_space=pltpu.SMEM)] + [pl.BlockSpec(memory_space=pltpu.HBM)] * 4,
        scratch_shapes=[
            pltpu.VMEM((4, TOK, 2 * HALF), BF16),
            pltpu.SemaphoreType.DMA((4, CUTS)),
        ],
        compiler_params=pltpu.CompilerParams(vmem_limit_bytes=62 * 1024 * 1024),
    )(core.reshape(1), q_raw, k_raw, v_in, cotangent)
    totals = sum_heads(sums)
    got = other_core(send)
    second_group = lambda both: jnp.where(first, both[TOK:], both[:TOK])
    v2 = jnp.concatenate([keep[2], got[2]], axis=0)
    v_prev = move_chips(v2, line_shift(1))
    tags = jnp.concatenate(
        [totals, frame_index.astype(F32)[None], jnp.broadcast_to(reach.astype(F32), (1, TOK))]
    )
    tags_got = other_core(tags)
    pick = lambda value: jnp.where(first, value[:HALF], value[HALF:])[None, :]
    gains_q, gains_k = pick(gain_q), pick(gain_k)
    quarter = shape(QUARTER, 2 * HALF, kind=BF16)
    q_norm, k_norm, bias, *quarters = call(
        norm_kernel,
        (low_half(2 * TOK), low_half(2 * TOK), shape(2 * TOK, KEYS)) + (quarter,) * XS,
        scalar=True,
        args=6,
    )(places, keep, got, tags, tags_got, gains_q, gains_k)
    parts = [quarters[0]] + [
        move_chips(part, pairs_of(turn)) for part, turn in zip(quarters[1:], SCATTER_X)
    ]
    low, k_sent, v_prev = after((add_parts(*parts), k_norm, v_prev))
    k_prev = move_chips(k_sent, line_shift(1))
    low = add_parts(low, *rounds(SPREAD_Z[0], low))
    low, v_prev = after((low, v_prev))
    v_early = move_chips(second_group(v_prev), line_shift(1))
    low = add_parts(low, *rounds(SPREAD_Z[1], low))
    low, k_prev = after((low, k_prev))
    k_early = move_chips(second_group(k_prev), line_shift(1))
    parts = [low] + [shift_x(low, by) for by in (1, 2, 3)]
    blocks = (k_norm, k_prev, k_early, v2, v_prev, v_early)

    attn, top, probs, sink = call(
        forward_kernel,
        (
            low_half(2 * TOK),
            shape(1, HALF),
            shape(HEADS, 2 * TOK, KEYS, kind=BF16),
            shape(TOK, 2 * HALF, kind=BF16),
        ),
        2 * block_flops,
        6 * 1024 * 1024,
        HEADS * 2 * TOK * KEYS,
        scalar=True,
        args=12,
    )(places, bias, q_norm, *blocks, *parts)

    pair = pairs_z(top, jnp.maximum)
    v_own, v_prev_out, v_early_out, v_low = call(
        value_kernel,
        (shape(2 * TOK, HALF), low_half(2 * TOK), low_half(TOK), low_half(TOK)),
        block_flops,
        4 * 1024 * 1024,
    )(probs, keep, got)
    pair, v_low, v_prev_out, v_early_out = after((pair, v_low, v_prev_out, v_early_out))
    v_near = move_chips(v_prev_out, line_shift(-1))
    quad = quads_z(pair, jnp.maximum)
    chan = quads_x(quad, jnp.maximum)
    chan, v_near = after((chan, v_near))

    low, grad_qn, k_own, k_prev_out, k_early_out, scaled, gain_sum, inner = call(
        backward_kernel,
        (
            shape(TOK, 2 * HALF, kind=BF16),
            shape(2 * TOK, HALF),
            shape(2 * TOK, HALF),
            low_half(2 * TOK),
            shape(TOK, 2 * HALF, kind=BF16),
            low_half(2 * TOK),
            shape(1, HALF),
            shape(3, TOK),
        ),
        3 * block_flops,
        8 * 1024 * 1024,
    )(probs, keep, got, attn, chan, q_norm, *blocks, sink, v_low, v_early_out)

    near = move_chips(k_prev_out, line_shift(-1))
    far = move_chips(k_early_out, line_shift(-2))
    from_x = rounds(GATHER_X, low)
    near, far, from_x = after((near, far, from_x))
    k_total, low, inner, swapped = call(
        key_sum_kernel,
        (
            shape(2 * TOK, HALF),
            shape(TOK, 2 * HALF, kind=BF16),
            shape(8, TOK),
            shape(8, TOK),
        ),
        scalar=True,
        args=9,
    )(places, k_own, near, far, k_norm, inner, low, *from_x)
    inner = sum_heads(inner + other_core(swapped))
    low = add_parts(low, *rounds(GATHER_Z[0], low))
    sums = jnp.concatenate([gain_sum.reshape(HEADS, HD), inner[4:5]])

    sums, low = after((sums, low))
    low = add_parts(low, *rounds(GATHER_Z[1], low))
    sums = quads_x(sums, jnp.add)
    sums = pairs_z(sums, jnp.add)
    sums, low = after((sums, low))
    sums = quads_z(sums, jnp.add)

    q_mine, q_other = call(query_kernel, (low_half(TOK), low_half(TOK)))(
        grad_qn, keep, got, tags, tags_got, gains_q, inner
    )
    both = shape(2, TOK, HALF, kind=BF16)
    mine, other = call(key_kernel, (both, both), scalar=True, args=13)(
        places, k_total, v_own, v_near, far, low, inner, sums[HEADS:], chan,
        keep, got, tags, tags_got, gains_k,
    )

    def cores_out(mine, other):
        theirs = other_core(other)
        return jnp.where(
            first,
            jnp.concatenate([mine, theirs], axis=-1),
            jnp.concatenate([theirs, mine], axis=-1),
        )

    scaled_out = cores_out(scaled[:TOK], scaled[TOK:])
    grad_q = cores_out(q_mine, q_other)
    theirs = other_core(other)
    join = lambda a, b: jnp.where(
        first, jnp.concatenate([a, b], axis=1), jnp.concatenate([b, a], axis=1)
    )
    grad_k = join(mine[0], theirs[0])
    grad_v = join(mine[1], theirs[1])
    gain_total = sums[:HEADS].reshape(1, HALF)
    gain_both = cores_out(gain_total, gain_total)[0]
    return (scaled_out, grad_q, grad_k, grad_v, gain_both / gain_q, gain_both / gain_k)


def solution(mesh):
    rows = P("frame", "head")
    placed = (rows, rows, rows, P("head"), P("head"), P("frame"), P("frame"), rows)
    return jax.shard_map(
        per_device,
        mesh=mesh,
        in_specs=placed,
        out_specs=(rows, rows, rows, rows, P("head"), P("head")),
        check_vma=False,
    )
```

```python
import jax
import jax.numpy as jnp
from jax import lax
from jax.experimental import pallas as pl
from jax.experimental.pallas import tpu as pltpu
from jax.sharding import PartitionSpec as P

D = 5120
HD = 128
XS = 4
ZS = 8
TOK = 128
HALF = 640
HEADS = HALF // HD
KEYS = 6 * TOK
QUARTER = TOK // XS
CUTS = 2
EPSILON = 1e-06
HIDDEN = -1e30
F32 = jnp.float32
BF16 = jnp.bfloat16


def chip_pairs(move):
    pairs = []
    for x in range(XS):
        for z in range(ZS):
            to = move(x, z)
            if to is not None:
                for core in range(2):
                    pairs.append(((x * ZS + z) * 2 + core, (to[0] * ZS + to[1]) * 2 + core))
    return pairs


def move_chips(value, move):
    return lax.ppermute(value, "frame", chip_pairs(move))


def line_shift(by):
    def move(x, z):
        chip = x * ZS + z + by
        return divmod(chip, ZS) if 0 <= chip < XS * ZS else None

    return move


def shift_x(value, by):
    return move_chips(value, lambda x, z: ((x + by) % XS, z))


def shift_z(value, by):
    return move_chips(value, lambda x, z: (x, (z + by) % ZS))


def swap_z(value, bit):
    return move_chips(value, lambda x, z: (x, z ^ bit))


def other_core(value):
    return lax.ppermute(value, "frame", [(i, i ^ 1) for i in range(2 * XS * ZS)])


def head_turns(value):
    return [lax.ppermute(value, "head", [(i, (i + by) % 4) for i in range(4)]) for by in (2, 1, 3)]


def sum_heads(value):
    turns = head_turns(value)
    return (value + turns[0]) + (turns[1] + turns[2])


def pairs_of(turn):
    return lambda x, z: turn.get((x, z))


def column(moves, xs):
    return {(x, a): (x, b) for x in xs for a, b in moves.items()}


def row(a, b, zs):
    return {(a, z): (b, z) for z in zs}


SCATTER_X = tuple(row(0, to, (0,)) for to in range(1, XS))
GATHER_X = tuple(row(src, 0, (0,)) for src in range(1, XS))
SPREAD_Z = (
    (column({0: 5}, range(XS)), column({0: 6}, range(XS))),
    (column({0: 7, 5: 3, 6: 4}, range(XS)), column({0: 1, 5: 2}, range(XS))),
)
GATHER_Z = (
    (column({1: 0, 4: 3, 6: 5}, range(XS)), column({7: 0, 2: 3}, range(XS))),
    (column({3: 0}, range(XS)), column({5: 0}, range(XS))),
)


def add_parts(*parts, moved=0):
    first = parts[0]
    return call(
        add_kernel,
        jax.ShapeDtypeStruct(first.shape, BF16),
        moved=moved or 2 * (len(parts) + 1) * first.size,
    )(*parts)


def rounds(turns, low):
    return [move_chips(low, pairs_of(turn)) for turn in turns]


def after(values, *others):
    return lax.optimization_barrier((values, others))[0]


def pairs_z(value, join):
    return join(value, swap_z(value, 1))


def quads_z(value, join):
    turns = [shift_z(value, by) for by in (4, 2, 6)]
    return join(join(value, turns[0]), join(turns[1], turns[2]))


def quads_x(value, join):
    turns = [shift_x(value, by) for by in (2, 1, 3)]
    return join(join(value, turns[0]), join(turns[1], turns[2]))


def contract(a, b, dims, **kw):
    return lax.dot_general(a, b, (dims, ((), ())), preferred_element_type=F32, **kw)


def lane_sums(block):
    ones = jnp.ones((8, HD), F32)
    return contract(ones, block, ((1,), (1,)), precision=lax.Precision.HIGHEST)[:1]


def upright(line):
    return jnp.broadcast_to(line, (TOK, TOK)).T[:, :1]


def fold(block):
    total = block[:, :HD]
    for start in range(HD, block.shape[1], HD):
        total = total + block[:, start : start + HD]
    return total


def entry_kernel(core, q, k, v, c, keep, send, sums, held, sems):
    step = TOK // CUTS
    copies = []
    for index, ref in enumerate((q, k, v, c)):
        for cut in range(CUTS):
            rows = pl.ds(cut * step, step)
            copies.append(
                pltpu.make_async_copy(ref.at[rows], held.at[index, rows], sems.at[index, cut])
            )
    for copy in copies:
        copy.start()
    mine = pl.ds(pl.multiple_of(core[0] * HALF, HD), HALF)
    other = pl.ds(pl.multiple_of((1 - core[0]) * HALF, HD), HALF)
    for index in range(4):
        for copy in copies[index * CUTS : (index + 1) * CUTS]:
            copy.wait()
        keep[index] = held[index, :, mine]
        send[index] = held[index, :, other]
        if index < 2:
            values = held[index].astype(F32)
            sums[index : index + 1] = lane_sums(fold(values * values))


def add_kernel(*refs):
    value = refs[0][...].astype(F32)
    for part in refs[1:-1]:
        value = value + part[...].astype(F32)
    refs[-1][...] = value.astype(BF16)


def norm_kernel(place, keep, got, tags, tags_got, gain_q, gain_k, q_norm, k_norm, bias, raw_k, *quarters):
    for half, (source, tag) in enumerate(((keep, tags), (got, tags_got))):
        rows = slice(half * TOK, (half + 1) * TOK)
        rate_q = upright(lax.rsqrt(tag[0:1] / D + EPSILON))
        rate_k = upright(lax.rsqrt(tag[1:2] / D + EPSILON))
        q_norm[rows] = (source[0].astype(F32) * rate_q * gain_q[...]).astype(BF16)
        raw_k[half] = source[1]
        k_norm[rows] = (source[1].astype(F32) * rate_k * gain_k[...]).astype(BF16)
    core = place[0] % 2

    def fill(source, start):
        for index, quarter in enumerate(quarters):
            rows = slice(index * QUARTER, (index + 1) * QUARTER)
            quarter[:, :HALF] = k_norm[start + rows.start : start + rows.stop]
            quarter[:, HALF:] = source[2, rows]

    @pl.when(core == 0)
    def _():
        fill(keep, 0)

    @pl.when(core == 1)
    def _():
        fill(got, TOK)

    @pl.when(place[0] >= 2)
    def _():
        quarters[0][...] = jnp.zeros((QUARTER, 2 * HALF), BF16)

    chip = place[0] // 2
    groups = (place[0], place[0] + 1 - 2 * core)
    ahead = 2 * chip - 2 + core
    key_groups = groups + (ahead, 4 * chip - 3 - ahead, 2 * chip - 3)
    nothing = jnp.zeros((TOK, TOK), F32)
    for half, tag in enumerate((tags, tags_got)):
        rows = slice(half * TOK, (half + 1) * TOK)
        frames = tag[2:3]
        reach = jnp.broadcast_to(tag[3:4], (TOK, TOK))
        for block in range(6):
            cols = slice(block * TOK, (block + 1) * TOK)
            if block == half:
                seen = frames <= upright(frames)
            elif block == 5:
                seen = reach < (nothing + groups[half].astype(F32))
            else:
                back = nothing + (groups[half] - key_groups[block]).astype(F32)
                seen = (back >= 1.0) & (back <= reach)
            bias[rows, cols] = jnp.where(seen, 0.0, HIDDEN)


def lanes_of(head):
    return slice(head * HD, (head + 1) * HD)


def key_rows(blocks, lanes):
    return jnp.concatenate([ref[:, lanes] for ref in blocks], axis=0)


def forward_kernel(
    place, bias, q, ko, kp, ke, vo, vp, ve, s0, s1, s2, s3, attn, top, probs, sink
):
    x = place[0] // (2 * ZS)
    for by, part in enumerate((s0, s1, s2, s3)):
        start = pl.multiple_of(((x + XS - by) % XS) * QUARTER, QUARTER)
        sink[pl.ds(start, QUARTER)] = part[...]
    for head in range(HEADS):
        lanes = lanes_of(head)
        keys = key_rows((ko, kp, ke, sink), lanes)
        values = jnp.concatenate(
            [key_rows((vo, vp, ve), lanes), sink[:, lanes_of(HEADS + head)]], axis=0
        )
        scores = contract(q[:, lanes], keys, ((1,), (1,))) * HD ** (-0.5) + bias[...]
        highest = jnp.max(scores, axis=1, keepdims=True)
        weights = jnp.exp(scores - highest)
        total = jnp.sum(weights, axis=1, keepdims=True)
        inverse = 1.0 / total
        summed = contract(weights.astype(BF16), values, ((1,), (0,)))
        rows = (summed * inverse).astype(BF16)
        attn[:, lanes] = rows
        top[:, lanes] = jnp.max(jnp.abs(rows.astype(F32)), axis=0, keepdims=True)
        probs[head] = (weights * inverse).astype(BF16)


def value_kernel(probs, keep, got, own, window, sink):
    for head in range(HEADS):
        lanes = lanes_of(head)
        cot = jnp.concatenate([keep[3, :, lanes], got[3, :, lanes]], axis=0)
        grads = contract(probs[head], cot, ((0,), (0,)))
        own[:, lanes] = grads[: 2 * TOK]
        window[:, lanes] = grads[2 * TOK : 5 * TOK].astype(BF16)
        sink[:, lanes] = grads[5 * TOK :].astype(BF16)


def backward_kernel(
    place, probs, keep, got, attn, chan, q, ko, kp, ke, vo, vp, ve, sink, v_low, v_relayed,
    p0, p1, p2, p3, grad_q, own, prev, early, scaled, gain_sum, inner, low,
):
    inner_q = jnp.zeros((2 * TOK, HD), F32)
    inner_sink = jnp.zeros((TOK, HD), F32)
    for head in range(HEADS):
        lanes = lanes_of(head)
        keys = jnp.concatenate([key_rows((ko, kp, ke), lanes), sink[:, lanes]], axis=0)
        values = jnp.concatenate(
            [key_rows((vo, vp, ve), lanes), sink[:, lanes_of(HEADS + head)]], axis=0
        )
        query = q[:, lanes]
        scale = chan[:, lanes] + EPSILON
        cot = jnp.concatenate([keep[3, :, lanes], got[3, :, lanes]], axis=0).astype(F32)
        grad_attn = (cot / scale).astype(BF16)
        out = attn[:, lanes].astype(F32)
        scaled[:, lanes] = (out / scale).astype(BF16)
        delta = jnp.sum(grad_attn.astype(F32) * out, axis=1, keepdims=True)
        grad_prob = contract(grad_attn, values, ((1,), (1,)))
        grad_score = (probs[head].astype(F32) * (grad_prob - delta)).astype(BF16)
        rows = contract(grad_score, keys, ((1,), (0,))) * HD ** (-0.5)
        grad_q[:, lanes] = rows
        product = rows * query.astype(F32)
        gain_sum[:, lanes] = jnp.sum(product, axis=0, keepdims=True)
        inner_q = inner_q + product
        grads = contract(grad_score, query, ((0,), (0,))) * HD ** (-0.5)
        inner_sink = inner_sink + grads[5 * TOK :] * keys[5 * TOK :].astype(F32)
        own[:, lanes] = grads[: 2 * TOK]
        prev[: 2 * TOK, lanes] = grads[2 * TOK : 4 * TOK].astype(BF16)
        early[:, lanes] = grads[4 * TOK : 5 * TOK].astype(BF16)
        low[:, lanes] = grads[5 * TOK :].astype(BF16)
    low[:, HALF:] = v_low[...]
    prev[2 * TOK :] = v_relayed[2 * TOK :]
    x = place[0] // (2 * ZS)
    for by, part in enumerate((p0, p1, p2, p3)):
        part[...] = low[pl.ds(pl.multiple_of(((x + by) % XS) * QUARTER, QUARTER), QUARTER)]
    inner[0:1] = lane_sums(inner_q[:TOK])
    inner[1:2] = lane_sums(inner_q[TOK:])
    inner[2:3] = lane_sums(inner_sink)


def key_sum_kernel(
    place, own, near, far, k_norm, inner, p0, p1, p2, p3, total, low, mine, other
):
    core = place[0] % 2
    rows = [inner[0:1], inner[1:2]]
    for half in range(2):
        part = slice(half * TOK, (half + 1) * TOK)
        use_far = jnp.where((core + half) == 1, 1.0, 0.0)
        grad = own[part] + near[part].astype(F32) + use_far * far[...].astype(F32)
        total[part] = grad
        rows.append(lane_sums(fold(grad * k_norm[part].astype(F32))))
    parts = (p0[...].astype(F32) + p1[...].astype(F32)) + (
        p2[...].astype(F32) + p3[...].astype(F32)
    )
    low[...] = parts.astype(BF16)
    rows.append(inner[2:3])
    for row, there in enumerate((1, 0, 3, 2, 4)):
        mine[row : row + 1] = rows[row]
        other[there : there + 1] = rows[row]
    mine[5:8] = jnp.zeros((3, TOK), F32)
    other[5:8] = jnp.zeros((3, TOK), F32)


def finish(grad, raw, rate, gains, inner):
    return (rate * gains * grad - raw.astype(F32) * (rate * rate * inner / D)).astype(BF16)


def query_kernel(grad, keep, got, tags, tags_got, gain_q, inner, mine, other):
    for half, (source, tag, out) in enumerate(((keep, tags, mine), (got, tags_got, other))):
        rows = slice(half * TOK, (half + 1) * TOK)
        rate = upright(lax.rsqrt(tag[0:1] / D + EPSILON))
        sums = upright(inner[half : half + 1])
        out[...] = finish(grad[rows], source[0], rate, gain_q[...], sums)


def key_kernel(
    place, k_total, v_own, v_near, near, s0, s1, s2, s3, inner, sink_inner, chan,
    raw_k, tags, tags_got, gain_k, mine, other,
):
    core = place[0] % 2
    scale = chan[...] + EPSILON
    sunk = jnp.concatenate([ref[...] for ref in (s0, s1, s2, s3)], axis=0)
    for half, (tag, out) in enumerate(((tags, mine), (tags_got, other))):
        rows = slice(half * TOK, (half + 1) * TOK)
        use_far = jnp.where((core + half) == 1, 1.0, 0.0)
        use_sink = jnp.where(place[0] < 2, 1.0, 0.0) * (1.0 - use_far)
        rate = upright(lax.rsqrt(tag[1:2] / D + EPSILON))
        grad = k_total[rows] + use_sink * sunk[:, :HALF].astype(F32)
        sums = upright(inner[2 + half : 3 + half] + use_sink * sink_inner[...])
        out[0] = finish(grad, raw_k[half], rate, gain_k[...], sums)
        grad = v_own[rows] + v_near[rows].astype(F32)
        grad = grad + use_far * near[2 * TOK :].astype(F32) + use_sink * sunk[:, HALF:].astype(F32)
        out[1] = (grad / scale).astype(BF16)


def shape(*dims, kind=F32):
    return jax.ShapeDtypeStruct(dims, kind)


def call(kernel, outs, flops=0, moved=2 * 1024 * 1024, exps=0, scalar=False, args=0):
    more = {}
    if scalar:
        more["in_specs"] = [pl.BlockSpec(memory_space=pltpu.SMEM)] + [
            pl.BlockSpec(memory_space=pltpu.VMEM)
        ] * args
    return pl.pallas_call(
        kernel,
        out_shape=outs,
        compiler_params=pltpu.CompilerParams(vmem_limit_bytes=20 * 1024 * 1024),
        cost_estimate=pl.CostEstimate(flops=flops, bytes_accessed=moved, transcendentals=exps),
        **more,
    )


def per_device(q_raw, k_raw, v_in, gain_q, gain_k, frame_index, reach, cotangent):
    place = lax.axis_index("frame")
    places = place.reshape(1)
    core = place % 2
    first = core == 0
    root = place < 2
    block_flops = 2 * 2 * TOK * KEYS * HALF
    low_half = lambda rows: shape(rows, HALF, kind=BF16)
    keep, send, sums = pl.pallas_call(
        entry_kernel,
        out_shape=(shape(4, TOK, HALF, kind=BF16),) * 2 + (shape(2, TOK),),
        in_specs=[pl.BlockSpec(memory_space=pltpu.SMEM)] + [pl.BlockSpec(memory_space=pltpu.HBM)] * 4,
        scratch_shapes=[
            pltpu.VMEM((4, TOK, 2 * HALF), BF16),
            pltpu.SemaphoreType.DMA((4, CUTS)),
        ],
        compiler_params=pltpu.CompilerParams(vmem_limit_bytes=62 * 1024 * 1024),
    )(core.reshape(1), q_raw, k_raw, v_in, cotangent)
    totals = sum_heads(sums)
    got = other_core(send)
    second_group = lambda both: jnp.where(first, both[TOK:], both[:TOK])
    v2 = jnp.concatenate([keep[2], got[2]], axis=0)
    v_prev = move_chips(v2, line_shift(1))
    tags = jnp.concatenate(
        [totals, frame_index.astype(F32)[None], jnp.broadcast_to(reach.astype(F32), (1, TOK))]
    )
    tags_got = other_core(tags)
    pick = lambda value: jnp.where(first, value[:HALF], value[HALF:])[None, :]
    gains_q, gains_k = pick(gain_q), pick(gain_k)
    quarter = shape(QUARTER, 2 * HALF, kind=BF16)
    q_norm, k_norm, bias, raw_k, *quarters = call(
        norm_kernel,
        (low_half(2 * TOK), low_half(2 * TOK), shape(2 * TOK, KEYS))
        + (shape(2, TOK, HALF, kind=BF16),)
        + (quarter,) * XS,
        scalar=True,
        args=6,
    )(places, keep, got, tags, tags_got, gains_q, gains_k)
    parts = [quarters[0]] + [
        move_chips(part, pairs_of(turn)) for part, turn in zip(quarters[1:], SCATTER_X)
    ]
    low, k_sent, v_prev = after((add_parts(*parts), k_norm, v_prev))
    k_prev = move_chips(k_sent, line_shift(1))
    low = add_parts(low, *rounds(SPREAD_Z[0], low))
    low, v_prev = after((low, v_prev))
    v_early = move_chips(second_group(v_prev), line_shift(1))
    low = add_parts(low, *rounds(SPREAD_Z[1], low))
    low, k_prev = after((low, k_prev))
    k_early = move_chips(second_group(k_prev), line_shift(1))
    parts = [low] + [shift_x(low, by) for by in (1, 2, 3)]
    blocks = (k_norm, k_prev, k_early, v2, v_prev, v_early)

    attn, top, probs, sink = call(
        forward_kernel,
        (
            low_half(2 * TOK),
            shape(1, HALF),
            shape(HEADS, 2 * TOK, KEYS, kind=BF16),
            shape(TOK, 2 * HALF, kind=BF16),
        ),
        2 * block_flops,
        6 * 1024 * 1024,
        HEADS * 2 * TOK * KEYS,
        scalar=True,
        args=12,
    )(places, bias, q_norm, *blocks, *parts)

    pair = pairs_z(top, jnp.maximum)
    v_own, v_window, v_low = call(
        value_kernel,
        (shape(2 * TOK, HALF), low_half(3 * TOK), low_half(TOK)),
        block_flops,
        4 * 1024 * 1024,
    )(probs, keep, got)
    pair, v_low, v_window = after((pair, v_low, v_window))
    v_near = move_chips(v_window, line_shift(-1))
    quad = quads_z(pair, jnp.maximum)
    chan = quads_x(quad, jnp.maximum)
    chan, v_near = after((chan, v_near))

    vmem = pl.BlockSpec(memory_space=pltpu.VMEM)
    *pieces, grad_qn, k_own, k_prev_out, k_early_out, scaled, gain_sum, inner = pl.pallas_call(
        backward_kernel,
        out_shape=(quarter,) * XS
        + (
            shape(2 * TOK, HALF),
            shape(2 * TOK, HALF),
            low_half(3 * TOK),
            low_half(TOK),
            low_half(2 * TOK),
            shape(1, HALF),
            shape(3, TOK),
        ),
        in_specs=[pl.BlockSpec(memory_space=pltpu.SMEM)] + [vmem] * 15,
        scratch_shapes=[pltpu.VMEM((TOK, 2 * HALF), BF16)],
        compiler_params=pltpu.CompilerParams(vmem_limit_bytes=20 * 1024 * 1024),
        cost_estimate=pl.CostEstimate(
            flops=3 * block_flops, bytes_accessed=8 * 1024 * 1024, transcendentals=0
        ),
    )(places, probs, keep, got, attn, chan, q_norm, *blocks, sink, v_low, v_near)

    near = move_chips(k_prev_out, line_shift(-1))
    far = move_chips(k_early_out, line_shift(-2))
    from_x = [pieces[0]] + [shift_x(pieces[by], by) for by in (1, 2, 3)]
    near, far, from_x = after((near, far, from_x))
    k_total, low, inner, swapped = call(
        key_sum_kernel,
        (
            shape(2 * TOK, HALF),
            quarter,
            shape(8, TOK),
            shape(8, TOK),
        ),
        scalar=True,
        args=9,
    )(places, k_own, near, far, k_norm, inner, *from_x)
    inner = sum_heads(inner + other_core(swapped))
    low = add_parts(low, *rounds(GATHER_Z[0], low))
    sums = jnp.concatenate([gain_sum.reshape(HEADS, HD), inner[4:5]])

    sums, low = after((sums, low))
    low = add_parts(low, *rounds(GATHER_Z[1], low))
    sums = quads_x(sums, jnp.add)
    sums = pairs_z(sums, jnp.add)
    sums, low = after((sums, low))
    sunk = [low] + rounds(GATHER_X, low)
    turns = [shift_z(sums, by) for by in (4, 2, 6)]
    sums, turns, sunk = after((sums, turns, sunk))
    sums = (sums + turns[0]) + (turns[1] + turns[2])

    q_mine, q_other = call(query_kernel, (low_half(TOK), low_half(TOK)))(
        grad_qn, keep, got, tags, tags_got, gains_q, inner
    )
    both = shape(2, TOK, HALF, kind=BF16)
    mine, other = call(key_kernel, (both, both), scalar=True, args=15)(
        places, k_total, v_own, v_near, near, *sunk, inner, sums[HEADS:], chan,
        raw_k, tags, tags_got, gains_k,
    )

    def cores_out(mine, other):
        theirs = other_core(other)
        return jnp.where(
            first,
            jnp.concatenate([mine, theirs], axis=-1),
            jnp.concatenate([theirs, mine], axis=-1),
        )

    scaled_out = cores_out(scaled[:TOK], scaled[TOK:])
    grad_q = cores_out(q_mine, q_other)
    theirs = other_core(other)
    join = lambda a, b: jnp.where(
        first, jnp.concatenate([a, b], axis=1), jnp.concatenate([b, a], axis=1)
    )
    grad_k = join(mine[0], theirs[0])
    grad_v = join(mine[1], theirs[1])
    gain_total = sums[:HEADS].reshape(1, HALF)
    gain_both = cores_out(gain_total, gain_total)[0]
    return (scaled_out, grad_q, grad_k, grad_v, gain_both / gain_q, gain_both / gain_k)


def solution(mesh):
    rows = P("frame", "head")
    placed = (rows, rows, rows, P("head"), P("head"), P("frame"), P("frame"), rows)
    return jax.shard_map(
        per_device,
        mesh=mesh,
        in_specs=placed,
        out_specs=(rows, rows, rows, rows, P("head"), P("head")),
        check_vma=False,
    )
```

```python
import jax
import jax.numpy as jnp
from jax import lax
from jax.experimental import pallas as pl
from jax.experimental.pallas import tpu as pltpu
from jax.sharding import PartitionSpec as P

D = 5120
HD = 128
XS = 4
ZS = 8
TOK = 128
HALF = 640
HEADS = HALF // HD
KEYS = 6 * TOK
QUARTER = TOK // XS
CUTS = 2
EPSILON = 1e-06
HIDDEN = -1e30
F32 = jnp.float32
BF16 = jnp.bfloat16


def chip_pairs(move):
    pairs = []
    for x in range(XS):
        for z in range(ZS):
            to = move(x, z)
            if to is not None:
                for core in range(2):
                    pairs.append(((x * ZS + z) * 2 + core, (to[0] * ZS + to[1]) * 2 + core))
    return pairs


def move_chips(value, move):
    return lax.ppermute(value, "frame", chip_pairs(move))


def line_shift(by):
    def move(x, z):
        chip = x * ZS + z + by
        return divmod(chip, ZS) if 0 <= chip < XS * ZS else None

    return move


def shift_x(value, by):
    return move_chips(value, lambda x, z: ((x + by) % XS, z))


def shift_z(value, by):
    return move_chips(value, lambda x, z: (x, (z + by) % ZS))


def swap_z(value, bit):
    return move_chips(value, lambda x, z: (x, z ^ bit))


def other_core(value):
    return lax.ppermute(value, "frame", [(i, i ^ 1) for i in range(2 * XS * ZS)])


def head_turns(value):
    return [lax.ppermute(value, "head", [(i, (i + by) % 4) for i in range(4)]) for by in (2, 1, 3)]


def sum_heads(value):
    turns = head_turns(value)
    return (value + turns[0]) + (turns[1] + turns[2])


def pairs_of(turn):
    return lambda x, z: turn.get((x, z))


def column(moves, xs):
    return {(x, a): (x, b) for x in xs for a, b in moves.items()}


def row(a, b, zs):
    return {(a, z): (b, z) for z in zs}


SCATTER_X = tuple(row(0, to, (0,)) for to in range(1, XS))
GATHER_X = tuple(row(src, 0, (0,)) for src in range(1, XS))
SPREAD_Z = (
    (column({0: 5}, range(XS)), column({0: 6}, range(XS))),
    (column({0: 1, 5: 3, 6: 7}, range(XS)), column({0: 2, 5: 4}, range(XS))),
)
GATHER_Z = (
    (column({1: 0, 4: 3, 6: 5}, range(XS)), column({7: 0, 2: 3}, range(XS))),
    (column({3: 0}, range(XS)), column({5: 0}, range(XS))),
)


def add_parts(*parts, moved=0):
    first = parts[0]
    return call(
        add_kernel,
        jax.ShapeDtypeStruct(first.shape, BF16),
        moved=moved or 2 * (len(parts) + 1) * first.size,
    )(*parts)


def rounds(turns, low):
    return [move_chips(low, pairs_of(turn)) for turn in turns]


def after(values, *others):
    return lax.optimization_barrier((values, others))[0]


def pairs_z(value, join):
    return join(value, swap_z(value, 1))


def quads_z(value, join):
    turns = [shift_z(value, by) for by in (4, 2, 6)]
    return join(join(value, turns[0]), join(turns[1], turns[2]))


def quads_x(value, join):
    turns = [shift_x(value, by) for by in (2, 1, 3)]
    return join(join(value, turns[0]), join(turns[1], turns[2]))


def contract(a, b, dims, **kw):
    return lax.dot_general(a, b, (dims, ((), ())), preferred_element_type=F32, **kw)


def lane_sums(block):
    ones = jnp.ones((8, HD), F32)
    return contract(ones, block, ((1,), (1,)), precision=lax.Precision.HIGHEST)[:1]


def upright(line):
    return jnp.broadcast_to(line, (TOK, TOK)).T[:, :1]


def fold(block):
    total = block[:, :HD]
    for start in range(HD, block.shape[1], HD):
        total = total + block[:, start : start + HD]
    return total


def entry_kernel(core, q, k, v, c, keep, send, sums, held, sems):
    step = TOK // CUTS
    copies = []
    for index, ref in enumerate((q, k, v, c)):
        for cut in range(CUTS):
            rows = pl.ds(cut * step, step)
            copies.append(
                pltpu.make_async_copy(ref.at[rows], held.at[index, rows], sems.at[index, cut])
            )
    for copy in copies:
        copy.start()
    mine = pl.ds(pl.multiple_of(core[0] * HALF, HD), HALF)
    other = pl.ds(pl.multiple_of((1 - core[0]) * HALF, HD), HALF)
    for index in range(4):
        for copy in copies[index * CUTS : (index + 1) * CUTS]:
            copy.wait()
        keep[index] = held[index, :, mine]
        send[index] = held[index, :, other]
        if index < 2:
            values = held[index].astype(F32)
            sums[index : index + 1] = lane_sums(fold(values * values))


def add_kernel(*refs):
    value = refs[0][...].astype(F32)
    for part in refs[1:-1]:
        value = value + part[...].astype(F32)
    refs[-1][...] = value.astype(BF16)


def norm_kernel(place, keep, got, tags, tags_got, gain_q, gain_k, q_norm, k_norm, bias, raw_k, *quarters):
    for half, (source, tag) in enumerate(((keep, tags), (got, tags_got))):
        rows = slice(half * TOK, (half + 1) * TOK)
        rate_q = upright(lax.rsqrt(tag[0:1] / D + EPSILON))
        rate_k = upright(lax.rsqrt(tag[1:2] / D + EPSILON))
        q_norm[rows] = (source[0].astype(F32) * rate_q * gain_q[...]).astype(BF16)
        raw_k[half] = source[1]
        k_norm[rows] = (source[1].astype(F32) * rate_k * gain_k[...]).astype(BF16)
    core = place[0] % 2

    def fill(source, start):
        for index, quarter in enumerate(quarters):
            rows = slice(index * QUARTER, (index + 1) * QUARTER)
            quarter[:, :HALF] = k_norm[start + rows.start : start + rows.stop]
            quarter[:, HALF:] = source[2, rows]

    @pl.when(core == 0)
    def _():
        fill(keep, 0)

    @pl.when(core == 1)
    def _():
        fill(got, TOK)

    @pl.when(place[0] >= 2)
    def _():
        quarters[0][...] = jnp.zeros((QUARTER, 2 * HALF), BF16)

    chip = place[0] // 2
    groups = (place[0], place[0] + 1 - 2 * core)
    ahead = 2 * chip - 2 + core
    key_groups = groups + (ahead, 4 * chip - 3 - ahead, 2 * chip - 3)
    nothing = jnp.zeros((TOK, TOK), F32)
    for half, tag in enumerate((tags, tags_got)):
        rows = slice(half * TOK, (half + 1) * TOK)
        frames = tag[2:3]
        reach = jnp.broadcast_to(tag[3:4], (TOK, TOK))
        for block in range(6):
            cols = slice(block * TOK, (block + 1) * TOK)
            if block == half:
                seen = frames <= upright(frames)
            elif block == 5:
                seen = reach < (nothing + groups[half].astype(F32))
            else:
                back = nothing + (groups[half] - key_groups[block]).astype(F32)
                seen = (back >= 1.0) & (back <= reach)
            bias[rows, cols] = jnp.where(seen, 0.0, HIDDEN)


def lanes_of(head):
    return slice(head * HD, (head + 1) * HD)


def key_rows(blocks, lanes):
    return jnp.concatenate([ref[:, lanes] for ref in blocks], axis=0)


def forward_kernel(
    place, bias, q, ko, kp, ke, vo, vp, ve, s0, s1, s2, s3, attn, top, probs, sink
):
    x = place[0] // (2 * ZS)
    for by, part in enumerate((s0, s1, s2, s3)):
        start = pl.multiple_of(((x + XS - by) % XS) * QUARTER, QUARTER)
        sink[pl.ds(start, QUARTER)] = part[...]
    for head in range(HEADS):
        lanes = lanes_of(head)
        keys = key_rows((ko, kp, ke, sink), lanes)
        values = jnp.concatenate(
            [key_rows((vo, vp, ve), lanes), sink[:, lanes_of(HEADS + head)]], axis=0
        )
        scores = contract(q[:, lanes], keys, ((1,), (1,))) * HD ** (-0.5) + bias[...]
        highest = jnp.max(scores, axis=1, keepdims=True)
        weights = jnp.exp(scores - highest)
        total = jnp.sum(weights, axis=1, keepdims=True)
        inverse = 1.0 / total
        summed = contract(weights.astype(BF16), values, ((1,), (0,)))
        rows = (summed * inverse).astype(BF16)
        attn[:, lanes] = rows
        top[:, lanes] = jnp.max(jnp.abs(rows.astype(F32)), axis=0, keepdims=True)
        probs[head] = (weights * inverse).astype(BF16)


def value_kernel(probs, keep, got, own, window, sink):
    for head in range(HEADS):
        lanes = lanes_of(head)
        cot = jnp.concatenate([keep[3, :, lanes], got[3, :, lanes]], axis=0)
        grads = contract(probs[head], cot, ((0,), (0,)))
        own[:, lanes] = grads[: 2 * TOK]
        window[:, lanes] = grads[2 * TOK : 5 * TOK].astype(BF16)
        sink[:, lanes] = grads[5 * TOK :].astype(BF16)


def backward_kernel(
    place, probs, keep, got, attn, chan, q, ko, kp, ke, vo, vp, ve, sink, v_low, v_relayed,
    p0, p1, p2, p3, grad_q, own, prev, early, scaled, gain_sum, inner, low,
):
    inner_q = jnp.zeros((2 * TOK, HD), F32)
    inner_sink = jnp.zeros((TOK, HD), F32)
    for head in range(HEADS):
        lanes = lanes_of(head)
        keys = jnp.concatenate([key_rows((ko, kp, ke), lanes), sink[:, lanes]], axis=0)
        values = jnp.concatenate(
            [key_rows((vo, vp, ve), lanes), sink[:, lanes_of(HEADS + head)]], axis=0
        )
        query = q[:, lanes]
        scale = chan[:, lanes] + EPSILON
        cot = jnp.concatenate([keep[3, :, lanes], got[3, :, lanes]], axis=0).astype(F32)
        grad_attn = (cot / scale).astype(BF16)
        out = attn[:, lanes].astype(F32)
        scaled[:, lanes] = (out / scale).astype(BF16)
        delta = jnp.sum(grad_attn.astype(F32) * out, axis=1, keepdims=True)
        grad_prob = contract(grad_attn, values, ((1,), (1,)))
        grad_score = (probs[head].astype(F32) * (grad_prob - delta)).astype(BF16)
        rows = contract(grad_score, keys, ((1,), (0,))) * HD ** (-0.5)
        grad_q[:, lanes] = rows
        product = rows * query.astype(F32)
        gain_sum[:, lanes] = jnp.sum(product, axis=0, keepdims=True)
        inner_q = inner_q + product
        grads = contract(grad_score, query, ((0,), (0,))) * HD ** (-0.5)
        inner_sink = inner_sink + grads[5 * TOK :] * keys[5 * TOK :].astype(F32)
        own[:, lanes] = grads[: 2 * TOK]
        prev[: 2 * TOK, lanes] = grads[2 * TOK : 4 * TOK].astype(BF16)
        early[:, lanes] = grads[4 * TOK : 5 * TOK].astype(BF16)
        low[:, lanes] = grads[5 * TOK :].astype(BF16)
    low[:, HALF:] = v_low[...]
    prev[2 * TOK :] = v_relayed[2 * TOK :]
    x = place[0] // (2 * ZS)
    for by, part in enumerate((p0, p1, p2, p3)):
        part[...] = low[pl.ds(pl.multiple_of(((x + by) % XS) * QUARTER, QUARTER), QUARTER)]
    inner[0:1] = lane_sums(inner_q[:TOK])
    inner[1:2] = lane_sums(inner_q[TOK:])
    inner[2:3] = lane_sums(inner_sink)


def key_sum_kernel(
    place, own, near, far, k_norm, inner, p0, p1, p2, p3, total, low, mine, other
):
    core = place[0] % 2
    rows = [inner[0:1], inner[1:2]]
    for half in range(2):
        part = slice(half * TOK, (half + 1) * TOK)
        use_far = jnp.where((core + half) == 1, 1.0, 0.0)
        grad = own[part] + near[part].astype(F32) + use_far * far[...].astype(F32)
        total[part] = grad
        rows.append(lane_sums(fold(grad * k_norm[part].astype(F32))))
    parts = (p0[...].astype(F32) + p1[...].astype(F32)) + (
        p2[...].astype(F32) + p3[...].astype(F32)
    )
    low[...] = parts.astype(BF16)
    rows.append(inner[2:3])
    for row, there in enumerate((1, 0, 3, 2, 4)):
        mine[row : row + 1] = rows[row]
        other[there : there + 1] = rows[row]
    mine[5:8] = jnp.zeros((3, TOK), F32)
    other[5:8] = jnp.zeros((3, TOK), F32)


def finish(grad, raw, rate, gains, inner):
    return (rate * gains * grad - raw.astype(F32) * (rate * rate * inner / D)).astype(BF16)


def query_kernel(grad, keep, got, tags, tags_got, gain_q, inner, mine, other):
    for half, (source, tag, out) in enumerate(((keep, tags, mine), (got, tags_got, other))):
        rows = slice(half * TOK, (half + 1) * TOK)
        rate = upright(lax.rsqrt(tag[0:1] / D + EPSILON))
        sums = upright(inner[half : half + 1])
        out[...] = finish(grad[rows], source[0], rate, gain_q[...], sums)


def key_kernel(
    place, k_total, v_own, v_near, near, s0, s1, s2, s3, inner, sink_inner, chan,
    raw_k, tags, tags_got, gain_k, mine, other,
):
    core = place[0] % 2
    scale = chan[...] + EPSILON
    sunk = jnp.concatenate([ref[...] for ref in (s0, s1, s2, s3)], axis=0)
    for half, (tag, out) in enumerate(((tags, mine), (tags_got, other))):
        rows = slice(half * TOK, (half + 1) * TOK)
        use_far = jnp.where((core + half) == 1, 1.0, 0.0)
        use_sink = jnp.where(place[0] < 2, 1.0, 0.0) * (1.0 - use_far)
        rate = upright(lax.rsqrt(tag[1:2] / D + EPSILON))
        grad = k_total[rows] + use_sink * sunk[:, :HALF].astype(F32)
        sums = upright(inner[2 + half : 3 + half] + use_sink * sink_inner[...])
        out[0] = finish(grad, raw_k[half], rate, gain_k[...], sums)
        grad = v_own[rows] + v_near[rows].astype(F32)
        grad = grad + use_far * near[2 * TOK :].astype(F32) + use_sink * sunk[:, HALF:].astype(F32)
        out[1] = (grad / scale).astype(BF16)


def shape(*dims, kind=F32):
    return jax.ShapeDtypeStruct(dims, kind)


def call(kernel, outs, flops=0, moved=2 * 1024 * 1024, exps=0, scalar=False, args=0):
    more = {}
    if scalar:
        more["in_specs"] = [pl.BlockSpec(memory_space=pltpu.SMEM)] + [
            pl.BlockSpec(memory_space=pltpu.VMEM)
        ] * args
    return pl.pallas_call(
        kernel,
        out_shape=outs,
        compiler_params=pltpu.CompilerParams(vmem_limit_bytes=20 * 1024 * 1024),
        cost_estimate=pl.CostEstimate(flops=flops, bytes_accessed=moved, transcendentals=exps),
        **more,
    )


def per_device(q_raw, k_raw, v_in, gain_q, gain_k, frame_index, reach, cotangent):
    place = lax.axis_index("frame")
    places = place.reshape(1)
    core = place % 2
    first = core == 0
    root = place < 2
    block_flops = 2 * 2 * TOK * KEYS * HALF
    low_half = lambda rows: shape(rows, HALF, kind=BF16)
    keep, send, sums = pl.pallas_call(
        entry_kernel,
        out_shape=(shape(4, TOK, HALF, kind=BF16),) * 2 + (shape(2, TOK),),
        in_specs=[pl.BlockSpec(memory_space=pltpu.SMEM)] + [pl.BlockSpec(memory_space=pltpu.HBM)] * 4,
        scratch_shapes=[
            pltpu.VMEM((4, TOK, 2 * HALF), BF16),
            pltpu.SemaphoreType.DMA((4, CUTS)),
        ],
        compiler_params=pltpu.CompilerParams(vmem_limit_bytes=62 * 1024 * 1024),
    )(core.reshape(1), q_raw, k_raw, v_in, cotangent)
    totals = sum_heads(sums)
    got = other_core(send)
    second_group = lambda both: jnp.where(first, both[TOK:], both[:TOK])
    v2 = jnp.concatenate([keep[2], got[2]], axis=0)
    v_prev = move_chips(v2, line_shift(1))
    tags = jnp.concatenate(
        [totals, frame_index.astype(F32)[None], jnp.broadcast_to(reach.astype(F32), (1, TOK))]
    )
    tags_got = other_core(tags)
    pick = lambda value: jnp.where(first, value[:HALF], value[HALF:])[None, :]
    gains_q, gains_k = pick(gain_q), pick(gain_k)
    quarter = shape(QUARTER, 2 * HALF, kind=BF16)
    q_norm, k_norm, bias, raw_k, *quarters = call(
        norm_kernel,
        (low_half(2 * TOK), low_half(2 * TOK), shape(2 * TOK, KEYS))
        + (shape(2, TOK, HALF, kind=BF16),)
        + (quarter,) * XS,
        scalar=True,
        args=6,
    )(places, keep, got, tags, tags_got, gains_q, gains_k)
    parts = [quarters[0]] + [
        move_chips(part, pairs_of(turn)) for part, turn in zip(quarters[1:], SCATTER_X)
    ]
    low, k_sent, v_prev = after((add_parts(*parts), k_norm, v_prev))
    k_prev = move_chips(k_sent, line_shift(1))
    low = add_parts(low, *rounds(SPREAD_Z[0], low))
    low, v_prev = after((low, v_prev))
    v_early = move_chips(second_group(v_prev), line_shift(1))
    low = add_parts(low, *rounds(SPREAD_Z[1], low))
    low, k_prev = after((low, k_prev))
    k_early = move_chips(second_group(k_prev), line_shift(1))
    turns = {by: shift_x(low, by) for by in (1, 3, 2)}
    parts = [low, turns[1], turns[2], turns[3]]
    blocks = (k_norm, k_prev, k_early, v2, v_prev, v_early)

    attn, top, probs, sink = call(
        forward_kernel,
        (
            low_half(2 * TOK),
            shape(1, HALF),
            shape(HEADS, 2 * TOK, KEYS, kind=BF16),
            shape(TOK, 2 * HALF, kind=BF16),
        ),
        2 * block_flops,
        6 * 1024 * 1024,
        HEADS * 2 * TOK * KEYS,
        scalar=True,
        args=12,
    )(places, bias, q_norm, *blocks, *parts)

    pair = pairs_z(top, jnp.maximum)
    v_own, v_window, v_low = call(
        value_kernel,
        (shape(2 * TOK, HALF), low_half(3 * TOK), low_half(TOK)),
        block_flops,
        4 * 1024 * 1024,
    )(probs, keep, got)
    pair, v_low, v_window = after((pair, v_low, v_window))
    v_near = move_chips(v_window, line_shift(-1))
    quad = quads_z(pair, jnp.maximum)
    chan = quads_x(quad, jnp.maximum)
    chan, v_near = after((chan, v_near))

    vmem = pl.BlockSpec(memory_space=pltpu.VMEM)
    *pieces, grad_qn, k_own, k_prev_out, k_early_out, scaled, gain_sum, inner = pl.pallas_call(
        backward_kernel,
        out_shape=(quarter,) * XS
        + (
            shape(2 * TOK, HALF),
            shape(2 * TOK, HALF),
            low_half(3 * TOK),
            low_half(TOK),
            low_half(2 * TOK),
            shape(1, HALF),
            shape(3, TOK),
        ),
        in_specs=[pl.BlockSpec(memory_space=pltpu.SMEM)] + [vmem] * 15,
        scratch_shapes=[pltpu.VMEM((TOK, 2 * HALF), BF16)],
        compiler_params=pltpu.CompilerParams(vmem_limit_bytes=20 * 1024 * 1024),
        cost_estimate=pl.CostEstimate(
            flops=3 * block_flops, bytes_accessed=8 * 1024 * 1024, transcendentals=0
        ),
    )(places, probs, keep, got, attn, chan, q_norm, *blocks, sink, v_low, v_near)

    near = move_chips(k_prev_out, line_shift(-1))
    far = move_chips(k_early_out, line_shift(-2))
    from_x = [pieces[0]] + [shift_x(pieces[by], by) for by in (1, 2, 3)]
    near, far, from_x = after((near, far, from_x))
    k_total, low, inner, swapped = call(
        key_sum_kernel,
        (
            shape(2 * TOK, HALF),
            quarter,
            shape(8, TOK),
            shape(8, TOK),
        ),
        scalar=True,
        args=9,
    )(places, k_own, near, far, k_norm, inner, *from_x)
    inner = sum_heads(inner + other_core(swapped))
    low = add_parts(low, *rounds(GATHER_Z[0], low))
    sums = jnp.concatenate([gain_sum.reshape(HEADS, HD), inner[4:5]])

    sums, low = after((sums, low))
    low = add_parts(low, *rounds(GATHER_Z[1], low))
    sums = quads_x(sums, jnp.add)
    sums = pairs_z(sums, jnp.add)
    sums, low = after((sums, low))
    sunk = [low] + rounds(GATHER_X, low)
    turns = [shift_z(sums, by) for by in (4, 2, 6)]
    sums, turns, sunk = after((sums, turns, sunk))
    sums = (sums + turns[0]) + (turns[1] + turns[2])

    q_mine, q_other = call(query_kernel, (low_half(TOK), low_half(TOK)))(
        grad_qn, keep, got, tags, tags_got, gains_q, inner
    )
    both = shape(2, TOK, HALF, kind=BF16)
    mine, other = call(key_kernel, (both, both), scalar=True, args=15)(
        places, k_total, v_own, v_near, near, *sunk, inner, sums[HEADS:], chan,
        raw_k, tags, tags_got, gains_k,
    )

    def cores_out(mine, other):
        theirs = other_core(other)
        return jnp.where(
            first,
            jnp.concatenate([mine, theirs], axis=-1),
            jnp.concatenate([theirs, mine], axis=-1),
        )

    scaled_out = cores_out(scaled[:TOK], scaled[TOK:])
    grad_q = cores_out(q_mine, q_other)
    theirs = other_core(other)
    join = lambda a, b: jnp.where(
        first, jnp.concatenate([a, b], axis=1), jnp.concatenate([b, a], axis=1)
    )
    grad_k = join(mine[0], theirs[0])
    grad_v = join(mine[1], theirs[1])
    gain_total = sums[:HEADS].reshape(1, HALF)
    gain_both = cores_out(gain_total, gain_total)[0]
    return (scaled_out, grad_q, grad_k, grad_v, gain_both / gain_q, gain_both / gain_k)


def solution(mesh):
    rows = P("frame", "head")
    placed = (rows, rows, rows, P("head"), P("head"), P("frame"), P("frame"), rows)
    return jax.shard_map(
        per_device,
        mesh=mesh,
        in_specs=placed,
        out_specs=(rows, rows, rows, rows, P("head"), P("head")),
        check_vma=False,
    )
```
